256 devices in a mesh: section: 4 (over x), tp: 16 (over z, core), dp: 4 (over y).
Axes of the slice: x: 4, y: 4, z: 8, core: 2. Of those that a mesh axis runs over, the one named last changes fastest.
Arguments:
- hidden_states: bfloat16 [672, 8192], P(None, 'dp'), may hold values from -120 to 120
- norm_gain: float32 [8192], P('dp'), may hold values from 0.5 to 1.5
- lm_head: bfloat16 [8192, 152064], P('dp', ('section', 'tp')), may hold values from -6 to 6
- target_ids: int32 [672], replicated, may hold values from 0 to 152063
Outputs:
- logprobs: bfloat16 [672, 152064], P(None, ('section', 'tp', 'dp'))
- target_logprob: float32 [672], P('dp')
The draws below stay inside these ranges and needn't reach their ends.
All inputs are finite; a program needn't handle non-finite values.
Results may differ from the reference program's by a relative error of at most 0.0031.
Values may be sent and summed in bfloat16 or wider, within the bound.
No kernel may reach another device: no remote copies, remote signals or barrier semaphores. Data moves between devices by JAX's collectives and lax.ppermute only.
A program may use at most 128 MiB of HBM per device.

```python
import math
import jax
import jax.numpy as jnp
import numpy as np
from jax import lax

D = 8192
ROWS = 672
VOCAB = 152064


def draw_hidden_states(key, part):
    key = jax.random.fold_in(key, 5)
    k_base, k_col, k_row = jax.random.split(key, 3)
    position = jnp.arange(D, dtype=jnp.float32) / D
    column = jnp.exp(0.55 * position) * jax.random.uniform(k_col, (D,), jnp.float32, 0.5, 1.5)
    row_scale = jnp.exp(jax.random.uniform(k_row, (ROWS, 1), jnp.float32, 0.0, 2.3))
    values = jax.random.truncated_normal(k_base, -4.0, 4.0, (ROWS, D), jnp.float32)
    return (values * column[None, :] * row_scale).astype(jnp.bfloat16)


def draw_lm_head(key, part):
    key = jax.random.fold_in(key, 9)
    k_base, k_col = jax.random.split(key, 2)
    position = jnp.arange(VOCAB, dtype=jnp.float32) / VOCAB
    column = 3.2 * (1.0 + 0.15 * position) * jax.random.uniform(k_col, (VOCAB,), jnp.float32, 0.6, 1.3)
    values = jax.random.truncated_normal(k_base, -4.0, 4.0, (D, VOCAB), jnp.float32) * column[None, :] / math.sqrt(D)
    return values.astype(jnp.bfloat16)


def set_ends(result, key, low, largest):
    longest = result.shape.index(max(result.shape))
    spots = []
    for shift in (0, 1):
        where = [jax.random.randint(jax.random.fold_in(key, axis), (), 0, length) for axis, length in enumerate(result.shape)]
        where[longest] = (where[longest] + shift) % result.shape[longest]
        spots.append(tuple(where))
    return result.at[spots[0]].set(low).at[spots[1]].set(largest)


def skewed_wide(own_key, shape, count, skew):
    loads = [min(1 << octave, count + 1 - (1 << octave)) * (1 << 20) // math.isqrt((1 << octave) ** skew) + 1 for octave in range((count + 1).bit_length()) if 1 << octave <= count]
    width = 1 + sum(loads) // (1 << 30)
    grid = np.cumsum(np.array([max(1, weight // width) for weight in loads]))
    lot = jax.random.randint(jax.random.fold_in(own_key, 1), shape, 0, int(grid[len(loads) - 1]))
    start = jnp.left_shift(1, jnp.searchsorted(jnp.asarray(grid, jnp.int32), lot, side="right").astype(jnp.int32))
    standing = start - 1 + jax.random.randint(jax.random.fold_in(own_key, 4), shape, 0, 1 << 30) % jnp.minimum(start, count + 1 - start)
    return jax.random.permutation(jax.random.fold_in(own_key, 2), count)[standing].astype(jnp.int32)


def setup_inputs(seed: int = 0) -> dict:
    splits = jax.random.split(jax.random.key(seed), 5)
    return {
        "hidden_states": draw_hidden_states(jax.random.fold_in(splits[4], 71), 0),
        "norm_gain": jnp.clip(1.0 + 0.1 * jax.random.normal(splits[1], (D,), jnp.float32), 0.5, 1.5),
        "lm_head": draw_lm_head(jax.random.fold_in(splits[4], 71), 0),
        "target_ids": set_ends(skewed_wide(splits[3], (ROWS,), VOCAB, 2), jax.random.fold_in(splits[3], 3), 0, VOCAB - 1).astype(jnp.int32),
    }


def reference(hidden_states, norm_gain, lm_head, target_ids):
    widened = hidden_states.astype(jnp.float32)
    mean_square = lax.optimization_barrier(jnp.mean(widened * widened, axis=1, keepdims=True))
    normed = (widened * lax.rsqrt(mean_square + 1e-06) * norm_gain[None, :]).astype(jnp.bfloat16)
    logits = jnp.dot(normed, lm_head, preferred_element_type=jnp.float32)
    row_top = lax.optimization_barrier(jnp.max(logits, axis=1, keepdims=True))
    row_total = lax.optimization_barrier(jnp.sum(jnp.exp(logits - row_top), axis=1, keepdims=True))
    logprobs = (logits - row_top - jnp.log(row_total)).astype(jnp.bfloat16)
    picked = jnp.take_along_axis(logits, target_ids.astype(jnp.int32)[:, None], axis=1)[:, 0]
    target_logprob = picked - row_top[:, 0] - jnp.log(row_total[:, 0])
    return (logprobs, target_logprob)
```

```python
import functools

import jax
import jax.numpy as jnp
from jax import lax
from jax.experimental import pallas as pl
from jax.experimental.pallas import tpu as pltpu
from jax.sharding import PartitionSpec as P

D = 8192
EPSILON = 1e-06
ROWS = 672
HALF = ROWS // 2
DP = 4
OWN = 594
STEP = 592
TAIL = 16
WIDE = 640
SQUARES = STEP + 8 - 512
VMEM = pltpu.CompilerParams(vmem_limit_bytes=50 * 1024 * 1024)
F32 = jnp.float32
BF16 = jnp.bfloat16


def whole():
    return pl.BlockSpec(memory_space=pltpu.VMEM)


def lane_of(shape):
    return lax.broadcasted_iota(jnp.int32, shape, 1)


def with_squares(tile, total):
    lane = lane_of(tile.shape)
    high = total.astype(BF16).astype(F32)
    middle = (total - high).astype(BF16).astype(F32)
    low = total - high - middle
    terms = jnp.where(lane == SQUARES, high, jnp.where(lane == SQUARES + 1, middle, low))
    return jnp.where(lane < SQUARES, tile, jnp.where(lane < SQUARES + 3, terms, 0.0))


def squares_of(tile):
    lane = lane_of(tile.shape)
    held = (lane >= SQUARES) & (lane < SQUARES + 3)
    return jnp.sum(jnp.where(held, tile, 0.0), axis=1, keepdims=True)


def window_dots(left, w_ref, t_ref, store):
    contract = (((1,), (1,)), ((), ()))
    for begin in (0, 256):
        store(begin, lax.dot_general(left, w_ref[begin : begin + 256, :], contract, preferred_element_type=F32))
    last = jnp.concatenate([w_ref[512:STEP, :], t_ref[...], w_ref[0:32, :]], axis=0)
    store(512, lax.dot_general(left, last, contract, preferred_element_type=F32))


def first_kernel(d_ref, x_ref, g_ref, w_ref, t_ref, hg_ref, sq_ref, up_ref, down_ref):
    half = pl.program_id(0)

    def prepare(i, _):
        rows = pl.ds(pl.multiple_of(i * 16, 16), 16)
        x = x_ref[rows, :].astype(F32)
        hg_ref[rows, :] = (x * g_ref[...]).astype(BF16)
        sq_ref[rows, :] = jnp.broadcast_to(jnp.sum(x * x, axis=1, keepdims=True), (16, 128))
        return 0

    lax.fori_loop(0, HALF // 16, prepare, 0)

    def compute(out_ref):
        def store(begin, product):
            if begin == 512:
                product = with_squares(product, sq_ref[:, 0:1])
            out_ref[:, begin : begin + product.shape[1]] = product.astype(BF16)

        window_dots(hg_ref[...], w_ref, t_ref, store)

    pl.when(half == 0)(lambda: compute(up_ref))
    pl.when(half == 1)(lambda: compute(down_ref))


def rest_kernel(d_ref, hg_ref, sq_ref, w_ref, t_ref, up_ref, up_held_ref, down_ref, down_held_ref, own_ref, res_ref):
    j = pl.program_id(0)
    for half in (0, 1):
        rows = slice(half * HALF, half * HALF + HALF)

        def store(begin, product):
            if begin == 512:
                product = with_squares(product, sq_ref[rows, 0:1])
            res_ref[rows, begin : begin + product.shape[1]] = product

        window_dots(hg_ref[rows, :], w_ref, t_ref, store)

    @pl.when(j == 0)
    def _():
        up_held_ref[...] = res_ref[:HALF, :]
        up_ref[...] = res_ref[HALF:, :].astype(BF16)

    @pl.when(j == 1)
    def _():
        down_ref[...] = res_ref[:HALF, :].astype(BF16)
        down_held_ref[...] = res_ref[HALF:, :]

    @pl.when(j == 2)
    def _():
        own_ref[...] = res_ref[...]


def add_kernel(up_in_ref, up_held_ref, down_in_ref, down_held_ref, up_ref, down_ref):
    for in_ref, held_ref, out_ref in ((up_in_ref, up_held_ref, up_ref), (down_in_ref, down_held_ref, down_ref)):

        def add(i, _):
            rows = pl.ds(pl.multiple_of(i * 16, 16), 16)
            out_ref[rows, :512] = (held_ref[rows, :512] + in_ref[rows, :512].astype(F32)).astype(BF16)
            came = in_ref[rows, 512:].astype(F32)
            held = held_ref[rows, 512:]
            out_ref[rows, 512:] = with_squares(came + held, squares_of(came) + squares_of(held)).astype(BF16)
            return 0

        lax.fori_loop(0, HALF // 16, add, 0)


def to_lanes(column):
    n = column.shape[0]
    same = lax.broadcasted_iota(jnp.int32, (n, 128), 0) == lane_of((n, 128))
    return jnp.sum(jnp.where(same, column, 0.0), axis=0, keepdims=True)


def to_column(row, n=128):
    same = lax.broadcasted_iota(jnp.int32, (n, 128), 0) == lane_of((n, 128))
    return jnp.sum(jnp.where(same, row, 0.0), axis=1, keepdims=True)


def total_kernel(d_ref, base_ref, own_ref, up2_ref, up3_ref, down2_ref, down3_ref, ids_ref, logits_ref, out_ref, ids_col, lse_col, picked_col):
    shift = lax.rem(WIDE - (OWN - STEP) * d_ref[0], WIDE)
    for begin in range(0, ROWS, 128):
        n = min(128, ROWS - begin)
        row = ids_ref[:, begin : begin + n]
        same = lax.broadcasted_iota(jnp.int32, (n, n), 0) == lane_of((n, n))
        ids_col[begin : begin + n, :] = jnp.sum(jnp.where(same, row.astype(F32), 0.0), axis=1, keepdims=True)
    for start, left_ref, right_ref in ((0, up3_ref, down2_ref), (HALF, up2_ref, down3_ref)):

        def finish(i, _):
            part = pl.ds(pl.multiple_of(i * 16, 16), 16)
            rows = pl.ds(pl.multiple_of(start + i * 16, 16), 16)
            own, left, right = own_ref[rows, :], left_ref[part, :].astype(F32), right_ref[part, :].astype(F32)
            squares = squares_of(own[:, 512:]) + (squares_of(left[:, 512:]) + squares_of(right[:, 512:]))
            scale = lax.rsqrt(squares / D + EPSILON)
            logits = pltpu.roll((own + (left + right)) * scale, shift, 1)
            lane = lane_of(logits.shape)
            logits_ref[rows, :] = logits
            kept = jnp.where(lane < OWN, logits, -jnp.inf)
            top = jnp.max(kept, axis=1, keepdims=True)
            lse_col[rows, :] = top + jnp.log(jnp.sum(jnp.exp(kept - top), axis=1, keepdims=True))
            target = ids_col[rows, :].astype(jnp.int32) - base_ref[0]
            hit = (lane == target) & (lane < OWN)
            picked_col[rows, :] = jnp.sum(jnp.where(hit, logits, 0.0), axis=1, keepdims=True)
            return 0

        lax.fori_loop(0, HALF // 16, finish, 0)
    out_ref[...] = jnp.zeros(out_ref.shape, F32)
    for k, begin in enumerate(range(0, ROWS, 128)):
        n = min(128, ROWS - begin)
        for place, col in ((k, lse_col), (8 + k, picked_col)):
            row = to_lanes(col[begin : begin + n, :])
            out_ref[:, place : place + 1, :] = jnp.broadcast_to(row[None], (out_ref.shape[0], 1, 128))


def joined(parts_ref):
    lse = parts_ref[:, 0:8, :]
    top = jnp.max(lse, axis=0)
    return top + jnp.log(jnp.sum(jnp.exp(lse - top[None]), axis=0)), jnp.sum(parts_ref[:, 8:16, :], axis=0)


def join_kernel(parts_ref, out_ref):
    lse, picked = joined(parts_ref)
    out_ref[:, 0:8, :] = jnp.broadcast_to(lse[None], (out_ref.shape[0], 8, 128))
    out_ref[:, 8:16, :] = jnp.broadcast_to(picked[None], (out_ref.shape[0], 8, 128))


def last_kernel(d_ref, logits_ref, parts_ref, out_ref, target_ref, lse_col, target_col):
    lse, picked = joined(parts_ref)
    for k, begin in enumerate(range(0, ROWS, 128)):
        n = min(128, ROWS - begin)
        lse_col[begin : begin + n, :] = to_column(lse[k : k + 1, :], n)
        target_col[begin : begin + n, :] = to_column(picked[k : k + 1, :] - lse[k : k + 1, :], n)

    def write(i, _):
        rows = pl.ds(pl.multiple_of(i * 16, 16), 16)
        out_ref[rows, :] = (logits_ref[rows, :] - lse_col[rows, :])[:, :OWN].astype(BF16)
        return 0

    lax.fori_loop(0, ROWS // 16, write, 0)
    own = ROWS // DP
    first = pl.multiple_of(d_ref[0] * own, 8)
    target_ref[:, 0:128] = to_lanes(target_col[pl.ds(first, 128), :])
    target_ref[:, 128:own] = to_lanes(target_col[pl.ds(first + 128, own - 128), :])[:, : own - 128]


def shape(*dims, dtype=F32):
    return jax.ShapeDtypeStruct(dims, dtype)


def cost(flops, nbytes):
    return pl.CostEstimate(flops=flops, bytes_accessed=nbytes, transcendentals=0)


def body(hidden_states, norm_gain, lm_head, target_ids):
    width = hidden_states.shape[1]
    d = lax.axis_index("dp")
    group = lax.axis_index("section") * lax.axis_size("tp") + lax.axis_index("tp")
    dp = d.astype(jnp.int32).reshape(1)
    base = ((group * DP + d) * OWN).astype(jnp.int32).reshape(1)
    weights = lm_head.T
    gain = norm_gain.reshape(1, width)
    ids = target_ids.reshape(1, ROWS)

    def chunk(offsets):
        def at(j, d_ref):
            offset = offsets[-1]
            for k, value in enumerate(offsets[:-1]):
                offset = jnp.where(j == k, value, offset)
            return lax.rem(d_ref[0] + offset, DP)

        return [
            pl.BlockSpec((STEP, width), lambda j, d_ref: (at(j, d_ref), 0)),
            pl.BlockSpec((TAIL, width), lambda j, d_ref: ((at(j, d_ref) + 1) * (STEP // TAIL), 0)),
        ]

    def fixed(*dims):
        return pl.BlockSpec(dims, lambda j, d_ref: (0, 0))

    hg, sq, up1, down1 = pl.pallas_call(
        first_kernel,
        grid_spec=pltpu.PrefetchScalarGridSpec(
            num_scalar_prefetch=1,
            grid=(2,),
            in_specs=[pl.BlockSpec((HALF, width), lambda j, d_ref: (j, 0)), fixed(1, width)] + chunk((2,)),
            out_specs=[
                pl.BlockSpec((HALF, width), lambda j, d_ref: (j, 0)),
                pl.BlockSpec((HALF, 128), lambda j, d_ref: (j, 0)),
                fixed(HALF, WIDE),
                fixed(HALF, WIDE),
            ],
        ),
        out_shape=(
            shape(ROWS, width, dtype=BF16),
            shape(ROWS, 128),
            shape(HALF, WIDE, dtype=BF16),
            shape(HALF, WIDE, dtype=BF16),
        ),
        compiler_params=VMEM,
        cost_estimate=cost(2 * ROWS * WIDE * width, 9_000_000),
        name="first_window",
    )(dp, hidden_states, gain, weights, weights)

    up = [(i, (i + 1) % DP) for i in range(DP)]
    down = [(i, (i - 1) % DP) for i in range(DP)]
    up1_in = lax.ppermute(up1, "dp", up)
    down1_in = lax.ppermute(down1, "dp", down)

    up2, up_held, down2, down_held, own = pl.pallas_call(
        rest_kernel,
        grid_spec=pltpu.PrefetchScalarGridSpec(
            num_scalar_prefetch=1,
            grid=(3,),
            in_specs=[fixed(ROWS, width), fixed(ROWS, 128)] + chunk((1, 3, 0)),
            out_specs=[fixed(HALF, WIDE)] * 4 + [fixed(ROWS, WIDE)],
            scratch_shapes=[pltpu.VMEM((ROWS, WIDE), F32)],
        ),
        out_shape=(
            shape(HALF, WIDE, dtype=BF16),
            shape(HALF, WIDE),
            shape(HALF, WIDE, dtype=BF16),
            shape(HALF, WIDE),
            shape(ROWS, WIDE),
        ),
        compiler_params=VMEM,
        cost_estimate=cost(6 * ROWS * WIDE * width, 16_000_000),
        name="other_windows",
    )(dp, hg, sq, weights, weights)
    up2_in = lax.ppermute(up2, "dp", up)
    down2_in = lax.ppermute(down2, "dp", down)

    up3, down3 = pl.pallas_call(
        add_kernel,
        in_specs=[whole()] * 4,
        out_specs=[whole()] * 2,
        out_shape=(shape(HALF, WIDE, dtype=BF16), shape(HALF, WIDE, dtype=BF16)),
        compiler_params=VMEM,
        cost_estimate=cost(ROWS * WIDE, 3_500_000),
        name="add_passing",
    )(up1_in, up_held, down1_in, down_held)
    up3_in = lax.ppermute(up3, "dp", up)
    down3_in = lax.ppermute(down3, "dp", down)

    scalar = pl.BlockSpec(memory_space=pltpu.SMEM)
    near = lax.axis_size(("section", "dp"))
    logits, parts = pl.pallas_call(
        total_kernel,
        in_specs=[scalar, scalar] + [whole()] * 6,
        out_specs=[whole()] * 2,
        out_shape=(shape(ROWS, WIDE), shape(near, 16, 128)),
        scratch_shapes=[pltpu.VMEM((ROWS, 1), F32)] * 3,
        compiler_params=VMEM,
        name="row_totals",
    )(dp, base, own, up2_in, up3_in, down2_in, down3_in, ids)
    parts = lax.all_to_all(parts, ("section", "dp"), 0, 0, tiled=True)
    parts = pl.pallas_call(
        join_kernel,
        in_specs=[whole()],
        out_specs=whole(),
        out_shape=shape(lax.axis_size("tp"), 16, 128),
        compiler_params=VMEM,
        name="join_totals",
    )(parts)
    parts = lax.all_to_all(parts, "tp", 0, 0, tiled=True)
    logprobs, target = pl.pallas_call(
        last_kernel,
        in_specs=[scalar, whole(), whole()],
        out_specs=[whole()] * 2,
        out_shape=(shape(ROWS, OWN, dtype=BF16), shape(1, ROWS // DP)),
        scratch_shapes=[pltpu.VMEM((ROWS, 1), F32)] * 2,
        compiler_params=VMEM,
        name="log_probabilities",
    )(dp, logits, parts)
    return logprobs, target.reshape(ROWS // DP)


def solution(mesh):
    placed = (P(None, "dp"), P("dp"), P("dp", ("section", "tp")), P())
    return jax.shard_map(
        body,
        mesh=mesh,
        in_specs=placed,
        out_specs=(P(None, ("section", "tp", "dp")), P("dp")),
        check_vma=False,
    )
```

```python
import jax
import jax.numpy as jnp
from jax import lax
from jax.experimental import pallas as pl
from jax.experimental.pallas import tpu as pltpu
from jax.sharding import PartitionSpec as P

D = 8192
EPSILON = 1e-06
ROWS = 672
HALF = ROWS // 2
DP = 4
OWN = 594
STEP = 592
SPAN = 600
WIDE = 640
LAST = 512
BLOCK = 112
PIECE = 48
F32 = jnp.float32
BF16 = jnp.bfloat16
CONTRACT = (((1,), (1,)), ((), ()))


def whole():
    return pl.BlockSpec(memory_space=pltpu.VMEM)


def far():
    return pl.BlockSpec(memory_space=pltpu.HBM)


def vmem(mib):
    return pltpu.CompilerParams(vmem_limit_bytes=mib * 1024 * 1024)


def shape(*dims, dtype=F32):
    return jax.ShapeDtypeStruct(dims, dtype)


def cost(flops, nbytes):
    return pl.CostEstimate(flops=flops, bytes_accessed=nbytes, transcendentals=0)


def lane_of(dims):
    return lax.broadcasted_iota(jnp.int32, dims, 1)


def row_of(dims):
    return lax.broadcasted_iota(jnp.int32, dims, 0)


def to_lanes(column):
    dims = (column.shape[0], 128)
    return jnp.sum(jnp.where(row_of(dims) == lane_of(dims), column, 0.0), axis=0, keepdims=True)


def to_column(row, n=128):
    return jnp.sum(jnp.where(row_of((n, 128)) == lane_of((n, 128)), row, 0.0), axis=1, keepdims=True)


def lane_groups():
    return [(k, begin, min(128, ROWS - begin)) for k, begin in enumerate(range(0, ROWS, 128))]


def window_copy(w_ref, chunk, held_ref, sem):
    rows = pl.ds(pl.multiple_of(lax.rem(chunk, DP) * STEP, 16), SPAN)
    return pltpu.make_async_copy(w_ref.at[rows], held_ref.at[pl.ds(0, SPAN)], sem)


def dot(left, right):
    return lax.dot_general(left, right, CONTRACT, preferred_element_type=F32)


def with_squares(tile, total, place):
    lane = lane_of(tile.shape)
    high = total.astype(BF16).astype(F32)
    middle = (total - high).astype(BF16).astype(F32)
    terms = jnp.where(lane == place, high, jnp.where(lane == place + 1, middle, total - high - middle))
    return jnp.where(lane < place, tile, jnp.where(lane < place + 3, terms, 0.0))


def squares_of(tile, place):
    lane = lane_of(tile.shape)
    return jnp.sum(jnp.where((lane >= place) & (lane < place + 3), tile, 0.0), axis=1, keepdims=True)


def scaled(x, g_ref, hg_ref, sq_ref, at):
    for begin in range(at, at + HALF, PIECE):
        rows = slice(begin, begin + PIECE)
        total = jnp.zeros((PIECE, 128), F32)
        for k in range(0, x.shape[1], 128):
            part = x[rows, k : k + 128].astype(F32)
            hg_ref[rows, k : k + 128] = (part * g_ref[:, k : k + 128]).astype(BF16)
            total = total + part * part
        sq_ref[rows, :] = jnp.broadcast_to(jnp.sum(total, axis=1, keepdims=True), (PIECE, 128))


def put_window(out_ref, product, squares, place):
    out_ref[:, :LAST] = product[:, :LAST].astype(BF16)
    out_ref[:, LAST:] = with_squares(product[:, LAST:], squares, place).astype(BF16)


def first_kernel(x_ref, g_ref, w_ref, hg_ref, sq_ref, up_ref, down_ref, w_up_ref, w_down_ref, x_held, g_held, w_held, sem):
    g_copy = pltpu.make_async_copy(g_ref, g_held, sem.at[0])
    w_copy = window_copy(w_ref, lax.axis_index("dp") + 2, w_held, sem.at[1])
    later = [window_copy(w_ref, lax.axis_index("dp") + 1, w_up_ref, sem.at[2]), window_copy(w_ref, lax.axis_index("dp") + 3, w_down_ref, sem.at[5])]
    x_copies = []
    for half in (0, 1):
        rows = pl.ds(half * HALF, HALF)
        x_copies.append(pltpu.make_async_copy(x_ref.at[rows], x_held.at[rows], sem.at[3 + half]))
    for copy in [g_copy, x_copies[0], w_copy, x_copies[1]] + later:
        copy.start()
    g_copy.wait()
    x_copies[0].wait()
    scaled(x_held, g_held, hg_ref, sq_ref, 0)
    w_copy.wait()
    x_copies[1].wait()
    for half, out_ref in ((0, up_ref), (1, down_ref)):
        rows = slice(half * HALF, half * HALF + HALF)
        if half == 1:
            scaled(x_held, g_held, hg_ref, sq_ref, HALF)
        put_window(out_ref, dot(hg_ref[rows, :], w_held[...]), sq_ref[rows, :], SPAN - LAST)
    for copy in later:
        copy.wait()


def direct_kernel(hg_ref, sq_ref, w_up_ref, w_down_ref, up_ref, down_ref):
    for i, (held_ref, out_ref) in enumerate(((w_up_ref, up_ref), (w_down_ref, down_ref))):
        rows = slice(HALF - i * HALF, ROWS - i * HALF)
        shift = lax.rem(WIDE - (OWN - STEP) * lax.rem(lax.axis_index("dp") + 1 + 2 * i, DP), WIDE)
        product = pltpu.roll(dot(hg_ref[rows, :], held_ref[...]), shift, 1)
        put_window(out_ref, product, sq_ref[rows, :], OWN - LAST)


def passing_kernel(hg_ref, sq_ref, w_up_ref, w_down_ref, up_in_ref, down_in_ref, up_ref, down_ref):
    for i, (held_ref, in_ref, out_ref) in enumerate(((w_up_ref, up_in_ref, up_ref), (w_down_ref, down_in_ref, down_ref))):
        rows = slice(i * HALF, i * HALF + HALF)
        shift = lax.rem(WIDE - (OWN - STEP) * lax.rem(lax.axis_index("dp") + 1 + 2 * i, DP), WIDE)
        came = in_ref[...].astype(F32)
        total = sq_ref[rows, :] + squares_of(came[:, LAST:], SPAN - LAST)
        product = pltpu.roll(dot(hg_ref[rows, :], held_ref[...]) + came, shift, 1)
        put_window(out_ref, product, total, OWN - LAST)


def own_kernel(hg_ref, w_ref, own_ref, w_held, sem):
    copy = window_copy(w_ref, lax.axis_index("dp"), w_held, sem.at[0])
    copy.start()
    copy.wait()
    own_ref[...] = dot(hg_ref[...], w_held[...])


def part_kernel(ids_ref, sq_ref, own_ref, up_ref, down_ref, sum_ref, part_ref, target_ref):
    group = lax.axis_index("section") * lax.axis_size("tp") + lax.axis_index("tp")
    base = (group * DP + lax.axis_index("dp")) * OWN
    shift = lax.rem(WIDE - (OWN - STEP) * lax.axis_index("dp"), WIDE)
    for k, begin, n in lane_groups():
        same = row_of((n, n)) == lane_of((n, n))
        ids = jnp.sum(jnp.where(same, ids_ref[:, begin : begin + n].astype(F32), 0.0), axis=1, keepdims=True)
        target = ids.astype(jnp.int32) - base
        target_ref[begin : begin + n, :] = jnp.broadcast_to(jnp.where(target < OWN, target, -1), (n, 128))
    for begin in range(0, ROWS, BLOCK):
        rows = slice(begin, begin + BLOCK)
        part = slice(begin % HALF, begin % HALF + BLOCK)
        came = (down_ref if begin < HALF else up_ref)[part, :].astype(F32)
        sum_ref[rows, :] = pltpu.roll(own_ref[rows, :], shift, 1) + came
        part_ref[rows, :] = sq_ref[rows, :] + squares_of(came[:, LAST:], OWN - LAST)


def put_rows(out_ref, place, row):
    out_ref[:, place : place + 1, :] = jnp.broadcast_to(row[None], (out_ref.shape[0], 1, 128))


def total_kernel(sum_ref, part_ref, target_ref, up_ref, down_ref, logits_ref, out_ref, lse_col, picked_col):
    lane = lane_of((PIECE, 128))
    for begin in range(0, ROWS, PIECE):
        rows = slice(begin, begin + PIECE)
        part = slice(begin % HALF, begin % HALF + PIECE)
        came_ref = up_ref if begin < HALF else down_ref
        squares = part_ref[rows, :] + squares_of(came_ref[part, LAST:].astype(F32), OWN - LAST)
        scale, target = lax.rsqrt(squares / D + EPSILON), target_ref[rows, :]
        tiles = []
        for k in range(0, WIDE, 128):
            tile = (sum_ref[rows, k : k + 128] + came_ref[part, k : k + 128].astype(F32)) * scale
            logits_ref[rows, k : k + 128] = tile
            tiles.append(jnp.where(lane < OWN - k, tile, -jnp.inf) if k + 128 > OWN else tile)
        top = tiles[0]
        for tile in tiles[1:]:
            top = jnp.maximum(top, tile)
        top = jnp.max(top, axis=1, keepdims=True)
        total = picked = jnp.zeros((PIECE, 128), F32)
        for k, tile in enumerate(tiles):
            total = total + jnp.exp(tile - top)
            picked = picked + jnp.where(lane == target - 128 * k, tile, 0.0)
        lse_col[rows, :] = top + jnp.log(jnp.sum(total, axis=1, keepdims=True))
        picked_col[rows, :] = jnp.sum(picked, axis=1, keepdims=True)
    for k, begin, n in lane_groups():
        put_rows(out_ref, k, to_lanes(lse_col[begin : begin + n, :]))
    own = ROWS // DP
    for k in range(DP):
        for place, begin, n in ((6, k * own, 128), (7, k * own + 128, own - 128)):
            row = to_lanes(picked_col[begin : begin + n, :])
            for part in range(k, out_ref.shape[0], DP):
                out_ref[part, place : place + 1, :] = row


def joined(parts_ref):
    parts = parts_ref[...]
    top = jnp.max(parts, axis=0)
    return top + jnp.log(jnp.sum(jnp.exp(parts - top[None]), axis=0)), jnp.sum(parts, axis=0)


def join_kernel(parts_ref, out_ref):
    lse, picked = joined(parts_ref)
    both = jnp.where(row_of(lse.shape) < 6, lse, picked)
    out_ref[...] = jnp.broadcast_to(both[None], out_ref.shape)


def last_kernel(logits_ref, parts_ref, out_ref, target_ref, out_held, lse_col, out_sem):
    lse, picked = joined(parts_ref)
    copies = []
    for k, begin, n in lane_groups():
        rows = slice(begin, begin + n)
        column = to_column(lse[k : k + 1, :], n)
        lse_col[rows, :] = column
        out_held[rows, :] = (logits_ref[rows, :] - column)[:, :OWN].astype(BF16)
        copies.append(pltpu.make_async_copy(out_held.at[pl.ds(begin, n)], out_ref.at[pl.ds(begin, n)], out_sem.at[k]))
        copies[-1].start()
    own = ROWS // DP
    first = pl.multiple_of(lax.axis_index("dp") * own, 8)
    target_ref[:, 0:128] = picked[6:7, :] - to_lanes(lse_col[pl.ds(first, 128), :])
    target_ref[:, 128:own] = (picked[7:8, :] - to_lanes(lse_col[pl.ds(first + 128, own - 128), :]))[:, : own - 128]
    for copy in copies:
        copy.wait()


def body(hidden_states, norm_gain, lm_head, target_ids):
    width = hidden_states.shape[1]
    hidden_states = pltpu.with_memory_space_constraint(hidden_states, pltpu.HBM)
    weights = pltpu.with_memory_space_constraint(lm_head.T, pltpu.HBM)
    gain = pltpu.with_memory_space_constraint(norm_gain.reshape(1, width), pltpu.HBM)
    ids = target_ids.reshape(1, ROWS)
    sent = pltpu.VMEM((HALF, WIDE), BF16)
    window = pltpu.VMEM((WIDE, width), BF16)
    window_flops = 2 * ROWS * WIDE * width

    hg, sq, up1, down1, w_up, w_down = pl.pallas_call(
        first_kernel,
        in_specs=[far(), far(), far()],
        out_specs=[whole()] * 6,
        out_shape=(pltpu.VMEM((ROWS, width), BF16), pltpu.VMEM((ROWS, 128), F32), sent, sent, window, window),
        scratch_shapes=[
            pltpu.VMEM((ROWS, width), BF16),
            pltpu.VMEM((1, width), F32),
            window,
            pltpu.SemaphoreType.DMA((6,)),
        ],
        compiler_params=vmem(12),
        cost_estimate=cost(window_flops, 10_000_000),
        name="first_window",
    )(hidden_states, gain, weights)

    def shifted(array, k):
        return lax.ppermute(array, "dp", [(i, (i + k) % DP) for i in range(DP)])

    up1_in, down1_in = shifted(up1, 1), shifted(down1, -1)
    up2, down2 = pl.pallas_call(
        direct_kernel,
        in_specs=[whole()] * 4,
        out_specs=[whole()] * 2,
        out_shape=(sent, sent),
        compiler_params=vmem(8),
        cost_estimate=cost(window_flops, 10_000_000),
        name="direct_windows",
    )(hg, sq, w_up, w_down)
    up2_in, down2_in = shifted(up2, 1), shifted(down2, -1)
    up3, down3 = pl.pallas_call(
        passing_kernel,
        in_specs=[whole()] * 6,
        out_specs=[whole()] * 2,
        out_shape=(sent, sent),
        compiler_params=vmem(8),
        cost_estimate=cost(window_flops, 10_000_000),
        name="passing_windows",
    )(hg, sq, w_up, w_down, up1_in, down1_in)
    up3_in, down3_in = shifted(up3, 1), shifted(down3, -1)

    own = pl.pallas_call(
        own_kernel,
        in_specs=[whole(), far()],
        out_specs=whole(),
        out_shape=pltpu.VMEM((ROWS, WIDE), F32),
        scratch_shapes=[window, pltpu.SemaphoreType.DMA((1,))],
        compiler_params=vmem(8),
        cost_estimate=cost(window_flops, 6_000_000),
        name="own_window",
    )(hg, weights)
    sums, part, target = pl.pallas_call(
        part_kernel,
        in_specs=[whole()] * 5,
        out_specs=[whole()] * 3,
        out_shape=(pltpu.VMEM((ROWS, WIDE), F32), pltpu.VMEM((ROWS, 128), F32), pltpu.VMEM((ROWS, 128), jnp.int32)),
        compiler_params=vmem(10),
        cost_estimate=cost(4 * ROWS * WIDE, 5_000_000),
        name="own_and_direct",
    )(ids, sq, own, up2_in, down2_in)

    near = lax.axis_size(("section", "dp"))
    logits, parts = pl.pallas_call(
        total_kernel,
        in_specs=[whole()] * 5,
        out_specs=[whole()] * 2,
        out_shape=(pltpu.VMEM((ROWS, WIDE), F32), shape(near, 8, 128)),
        scratch_shapes=[pltpu.VMEM((ROWS, 1), F32)] * 2,
        compiler_params=vmem(12),
        name="row_totals",
    )(sums, part, target, up3_in, down3_in)
    parts = lax.all_to_all(parts, ("section", "dp"), 0, 0, tiled=True)
    parts = pl.pallas_call(
        join_kernel,
        in_specs=[whole()],
        out_specs=whole(),
        out_shape=shape(lax.axis_size("tp"), 8, 128),
        compiler_params=vmem(2),
        name="join_totals",
    )(parts)
    parts = lax.all_to_all(parts, "tp", 0, 0, tiled=True)
    logprobs, target = pl.pallas_call(
        last_kernel,
        in_specs=[whole(), whole()],
        out_specs=[far(), whole()],
        out_shape=(shape(ROWS, OWN, dtype=BF16), shape(1, ROWS // DP)),
        scratch_shapes=[pltpu.VMEM((ROWS, OWN), BF16), pltpu.VMEM((ROWS, 1), F32), pltpu.SemaphoreType.DMA((6,))],
        compiler_params=vmem(8),
        name="log_probabilities",
    )(logits, parts)
    return logprobs, target.reshape(ROWS // DP)


def solution(mesh):
    placed = (P(None, "dp"), P("dp"), P("dp", ("section", "tp")), P())
    return jax.shard_map(
        body,
        mesh=mesh,
        in_specs=placed,
        out_specs=(P(None, ("section", "tp", "dp")), P("dp")),
        check_vma=False,
    )
```

```python
import jax
import jax.numpy as jnp
from jax import lax
from jax.experimental import pallas as pl
from jax.experimental.pallas import tpu as pltpu
from jax.sharding import PartitionSpec as P

D = 8192
EPSILON = 1e-06
ROWS = 672
HALF = ROWS // 2
QUARTER = ROWS // 4
FREE = QUARTER - 128
EARLY = 240
DP = 4
OWN = 594
STEP = 592
SPAN = 600
WIDE = 640
LAST = 512
OVER = OWN - LAST
PLACE = 3 * OVER - 128
BLOCK = 112
PIECE = 48
F32 = jnp.float32
BF16 = jnp.bfloat16
CONTRACT = (((1,), (1,)), ((), ()))


def whole():
    return pl.BlockSpec(memory_space=pltpu.VMEM)


def far():
    return pl.BlockSpec(memory_space=pltpu.HBM)


def vmem(mib):
    return pltpu.CompilerParams(vmem_limit_bytes=mib * 1024 * 1024)


def shape(*dims, dtype=F32):
    return jax.ShapeDtypeStruct(dims, dtype)


def cost(flops, nbytes):
    return pl.CostEstimate(flops=flops, bytes_accessed=nbytes, transcendentals=0)


def lane_of(dims):
    return lax.broadcasted_iota(jnp.int32, dims, 1)


def row_of(dims):
    return lax.broadcasted_iota(jnp.int32, dims, 0)


def to_lanes(column, begin=0):
    dims = (column.shape[0], 128)
    return jnp.sum(jnp.where(row_of(dims) + begin == lane_of(dims), column, 0.0), axis=0, keepdims=True)


def to_column(row, n=128):
    return jnp.sum(jnp.where(row_of((n, 128)) == lane_of((n, 128)), row, 0.0), axis=1, keepdims=True)


def lane_groups():
    return [(k, begin, min(128, ROWS - begin)) for k, begin in enumerate(range(0, ROWS, 128))]


def window_copy(w_ref, chunk, held_ref, sem):
    rows = pl.ds(pl.multiple_of(lax.rem(chunk, DP) * STEP, 16), SPAN)
    return pltpu.make_async_copy(w_ref.at[rows], held_ref.at[pl.ds(0, SPAN)], sem)


def dot(left, right):
    return lax.dot_general(left, right, CONTRACT, preferred_element_type=F32)


def message(rows):
    return pltpu.VMEM((rows + rows // 6, LAST), BF16)


def pack(out_ref, logits, squares):
    n = logits.shape[0]
    third, sixth = n // 3, n // 6
    out_ref[:n, :] = logits[:, :LAST].astype(BF16)
    over = [logits[k * third : k * third + third, LAST:] for k in range(3)]
    lane = lane_of((third, 128))
    middle = pltpu.roll(over[1], OVER, 1)
    first = jnp.where(lane < OVER, over[0], middle)
    second = jnp.where(lane < 2 * OVER - 128, middle, pltpu.roll(over[2], 2 * OVER - 128, 1))
    for k in range(3):
        total = squares[k * third : k * third + third]
        high = total.astype(BF16).astype(F32)
        mid = (total - high).astype(BF16).astype(F32)
        for place, term in enumerate((high, mid, total - high - mid)):
            second = jnp.where(lane == PLACE + 3 * k + place, term, second)
    second = jnp.where(lane < PLACE + 9, second, 0.0)
    for i in (0, 1):
        for j, tile in enumerate((first, second)):
            begin = 256 * i + 128 * j
            out_ref[n:, begin : begin + 128] = tile[i * sixth : i * sixth + sixth].astype(BF16)


def unpack(in_ref, n):
    third = n // 3
    rest = in_ref[n : n + n // 6, :].astype(F32)
    first = jnp.concatenate([rest[:, 0:128], rest[:, 256:384]], axis=0)
    second = jnp.concatenate([rest[:, 128:256], rest[:, 384:512]], axis=0)
    lane = lane_of((third, 128))
    middle = jnp.where(lane < 128 - OVER, pltpu.roll(first, 128 - OVER, 1), pltpu.roll(second, 128 - OVER, 1))
    over = jnp.concatenate([first, middle, pltpu.roll(second, 2 * (128 - OVER), 1)], axis=0)
    squares = []
    for k in range(3):
        held = (lane >= PLACE + 3 * k) & (lane < PLACE + 3 * k + 3)
        squares.append(jnp.sum(jnp.where(held, second, 0.0), axis=1, keepdims=True))
    return over, jnp.concatenate(squares, axis=0)


def aligned(logits, offset):
    chunk = lax.rem(lax.axis_index("dp") + offset, DP)
    return pltpu.roll(logits, lax.rem(WIDE - (OWN - STEP) * chunk, WIDE), 1)


def scaled(x, g_ref, hg_ref, sq_ref, at):
    for begin in range(at, at + HALF, PIECE):
        rows = slice(begin, begin + PIECE)
        total = jnp.zeros((PIECE, 128), F32)
        for k in range(0, x.shape[1], 128):
            part = x[rows, k : k + 128].astype(F32)
            hg_ref[rows, k : k + 128] = (part * g_ref[:, k : k + 128]).astype(BF16)
            total = total + part * part
        sq_ref[rows, :] = jnp.broadcast_to(jnp.sum(total, axis=1, keepdims=True), (PIECE, 128))


def first_kernel(x_ref, g_ref, w_ref, hg_ref, sq_ref, up_ref, down_ref, x_held, g_held, w_held, sem):
    g_copy = pltpu.make_async_copy(g_ref, g_held, sem.at[0])
    w_copy = window_copy(w_ref, lax.axis_index("dp") + 2, w_held, sem.at[1])
    x_copies = []
    for half in (0, 1):
        rows = pl.ds(half * HALF, HALF)
        x_copies.append(pltpu.make_async_copy(x_ref.at[rows], x_held.at[rows], sem.at[2 + half]))
    for copy in [g_copy, *x_copies, w_copy]:
        copy.start()
    g_copy.wait()
    for half in (0, 1):
        x_copies[half].wait()
        scaled(x_held, g_held, hg_ref, sq_ref, half * HALF)
    w_copy.wait()
    for half, out_ref in ((0, up_ref), (1, down_ref)):
        rows = slice(half * HALF, half * HALF + HALF)
        pack(out_ref, aligned(dot(hg_ref[rows, :], w_held[...]), 2), sq_ref[rows, :])


def direct_kernel(hg_ref, sq_ref, w_ref, up_ref, down_ref, w_up_ref, w_down_ref, sem):
    copies = []
    for i, held_ref in enumerate((w_up_ref, w_down_ref)):
        copies.append(window_copy(w_ref, lax.axis_index("dp") + 1 + 2 * i, held_ref, sem.at[i]))
        copies[-1].start()
    for copy in copies:
        copy.wait()
    for i, (held_ref, out_ref) in enumerate(((w_up_ref, up_ref), (w_down_ref, down_ref))):
        rows = slice(HALF - i * HALF, ROWS - i * HALF)
        pack(out_ref, aligned(dot(hg_ref[rows, :], held_ref[...]), 1 + 2 * i), sq_ref[rows, :])


def passing_kernel(hg_ref, sq_ref, w_up_ref, w_down_ref, up_in_ref, down_in_ref, w_ref, *outs):
    outs, (w_own_ref, sem) = outs[:4], outs[4:]
    copy = window_copy(w_ref, lax.axis_index("dp"), w_own_ref, sem.at[0])
    copy.start()
    for i, (held_ref, in_ref) in enumerate(((w_up_ref, up_in_ref), (w_down_ref, down_in_ref))):
        rows = slice(i * HALF, i * HALF + HALF)
        over, squares = unpack(in_ref, HALF)
        came = jnp.concatenate([in_ref[:HALF, :].astype(F32), over], axis=1)
        total = sq_ref[rows, :] + squares
        logits = aligned(dot(hg_ref[rows, :], held_ref[...]), 1 + 2 * i) + came
        for k, part in ((0, slice(0, EARLY)), (1, slice(EARLY, HALF))):
            pack(outs[2 * k + i], logits[part], total[part])
    copy.wait()


def own_kernel(hg_ref, w_own_ref, own_ref):
    own_ref[...] = dot(hg_ref[...], w_own_ref[...])


def part_kernel(ids_ref, sq_ref, own_ref, up_ref, down_ref, sum_ref, part_ref, target_ref):
    group = lax.axis_index("section") * lax.axis_size("tp") + lax.axis_index("tp")
    base = (group * DP + lax.axis_index("dp")) * OWN
    for k, begin, n in lane_groups():
        same = row_of((n, n)) == lane_of((n, n))
        ids = jnp.sum(jnp.where(same, ids_ref[:, begin : begin + n].astype(F32), 0.0), axis=1, keepdims=True)
        target = ids.astype(jnp.int32) - base
        target_ref[begin : begin + n, :] = jnp.broadcast_to(jnp.where(target < OWN, target, -1), (n, 128))
    for half, came_ref in ((0, down_ref), (1, up_ref)):
        over, squares = unpack(came_ref, HALF)
        part_ref[half * HALF : half * HALF + HALF, :] = sq_ref[half * HALF : half * HALF + HALF, :] + squares
        for begin in range(0, HALF, BLOCK):
            rows, part = slice(half * HALF + begin, half * HALF + begin + BLOCK), slice(begin, begin + BLOCK)
            own = aligned(own_ref[rows, :], 0)
            sum_ref[rows, :LAST] = own[:, :LAST] + came_ref[part, :].astype(F32)
            sum_ref[rows, LAST:] = own[:, LAST:] + over[part]


def block_totals(at, n, sum_ref, part_ref, target_ref, came_ref, logits_ref, to, over_ref, scale_ref, lse_ref, picked_ref):
    over, squares = unpack(came_ref, n)
    over_ref[...] = over
    scale_ref[...] = lax.rsqrt((part_ref[at : at + n, :] + squares) / D + EPSILON)
    for begin in range(0, n, PIECE):
        rows, part, out = (slice(start + begin, start + begin + PIECE) for start in (at, 0, to))
        lane = lane_of((PIECE, 128))
        scale, target = scale_ref[part, :], target_ref[rows, :]
        tiles = []
        for k in range(0, WIDE, 128):
            came = over_ref[part, :] if k == LAST else came_ref[part, k : k + 128].astype(F32)
            tile = (sum_ref[rows, k : k + 128] + came) * scale
            logits_ref[out, k : k + 128] = tile
            tiles.append(jnp.where(lane < OVER, tile, -jnp.inf) if k == LAST else tile)
        top = tiles[0]
        for tile in tiles[1:]:
            top = jnp.maximum(top, tile)
        top = jnp.max(top, axis=1, keepdims=True)
        total = picked = jnp.zeros((PIECE, 128), F32)
        for k, tile in enumerate(tiles):
            total = total + jnp.exp(tile - top)
            picked = picked + jnp.where(lane == target - 128 * k, tile, 0.0)
        lse_ref[part, :] = top + jnp.log(jnp.sum(total, axis=1, keepdims=True))
        picked_ref[part, :] = jnp.sum(picked, axis=1, keepdims=True)


def totals_scratch(n):
    return [pltpu.VMEM((2, n, lanes), F32) for lanes in (128, 128, 1, 1)]


def early_kernel(sum_ref, part_ref, target_ref, up_ref, down_ref, logits_ref, out_ref, *scratch):
    out_ref[...] = jnp.zeros(out_ref.shape, F32)
    for half, came_ref in ((0, up_ref), (1, down_ref)):
        held = [ref.at[half] for ref in scratch]
        block_totals(half * HALF, EARLY, sum_ref, part_ref, target_ref, came_ref, logits_ref, half * EARLY, *held)
        for first, column in zip((4 * half, 8 + 4 * half), held[2:]):
            for k, (begin, end) in enumerate(((0, 128), (128, QUARTER), (QUARTER, EARLY))):
                out_ref[first + k : first + k + 1, :] = to_lanes(column[begin:end, :])


def late_kernel(sum_ref, part_ref, target_ref, up_ref, down_ref, early_ref, logits_ref, out_ref, *scratch):
    late = HALF - EARLY
    row = row_of(early_ref.shape)
    rows = early_ref[...]
    for half, came_ref in ((0, up_ref), (1, down_ref)):
        held = [ref.at[half] for ref in scratch]
        block_totals(half * HALF + EARLY, late, sum_ref, part_ref, target_ref, came_ref, logits_ref, half * late, *held)
        for first, column in zip((4 * half, 8 + 4 * half), held[2:]):
            begun = EARLY - QUARTER
            rows = jnp.where(row == first + 2, rows + to_lanes(column[: 128 - begun, :], begun), rows)
            rows = jnp.where(row == first + 3, to_lanes(column[128 - begun :, :]), rows)
    out_ref[...] = jnp.broadcast_to(rows[None], out_ref.shape)


def join_kernel(parts_ref, out_ref):
    lse = joined(parts_ref[:, :8, :])
    picked = jnp.sum(parts_ref[:, 8:, :], axis=0)
    row, lane = row_of((8, 128)), lane_of((8, 128))
    for k in range(DP):
        first, second = (jnp.broadcast_to(picked[2 * k + i : 2 * k + i + 1, :], (8, 128)) for i in (0, 1))
        both = jnp.where((row == 1) & (lane >= FREE), pltpu.roll(first, FREE, 1), lse)
        both = jnp.where((row == 3) & (lane >= FREE), pltpu.roll(first, 2 * FREE, 1), both)
        both = jnp.where((row == 5) & (lane >= FREE), pltpu.roll(second, FREE, 1), both)
        for part in range(k, out_ref.shape[0], DP):
            out_ref[part, :, :] = both


def joined(parts):
    top = jnp.max(parts, axis=0)
    return top + jnp.log(jnp.sum(jnp.exp(parts - top[None]), axis=0))


def last_kernel(early_ref, late_ref, parts_ref, out_ref, target_ref, out_held, lse_held, column_ref, out_sem):
    parts = parts_ref[...]
    lse = joined(parts)
    lse_held[...] = lse
    copies = []
    for half in (0, 1):
        for k, begin, n in ((0, 0, 128), (1, 128, FREE), (2, QUARTER, 128), (3, QUARTER + 128, FREE)):
            column_ref[half * HALF + begin : half * HALF + begin + n, :] = to_column(lse[4 * half + k : 4 * half + k + 1, :], n)
    for half in (0, 1):
        for begin, n, logits_ref in ((0, EARLY, early_ref), (EARLY, HALF - EARLY, late_ref)):
            for piece in range(0, n, PIECE):
                rows = slice(half * HALF + begin + piece, half * HALF + begin + piece + PIECE)
                logits = logits_ref[half * n + piece : half * n + piece + PIECE, :]
                out_held[rows, :] = (logits - column_ref[rows, :])[:, :OWN].astype(BF16)
            rows = pl.ds(half * HALF + begin, n)
            copies.append(pltpu.make_async_copy(out_held.at[rows], out_ref.at[rows], out_sem.at[len(copies)]))
            copies[-1].start()
    picked = jnp.sum(parts, axis=0)
    lane = lane_of((1, 128))
    first = jnp.where(lane < 128 - FREE, pltpu.roll(picked[1:2, :], 128 - FREE, 1), pltpu.roll(picked[3:4, :], 128 - 2 * FREE, 1))
    second = pltpu.roll(picked[5:6, :], 128 - FREE, 1)
    place = 2 * lax.axis_index("dp")
    target_ref[:, 0:128] = first - lse_held[pl.ds(place, 1), :]
    target_ref[:, 128:QUARTER] = (second - lse_held[pl.ds(place + 1, 1), :])[:, : QUARTER - 128]
    for copy in copies:
        copy.wait()


def body(hidden_states, norm_gain, lm_head, target_ids):
    width = hidden_states.shape[1]
    hidden_states = pltpu.with_memory_space_constraint(hidden_states, pltpu.HBM)
    weights = pltpu.with_memory_space_constraint(lm_head.T, pltpu.HBM)
    gain = pltpu.with_memory_space_constraint(norm_gain.reshape(1, width), pltpu.HBM)
    ids = target_ids.reshape(1, ROWS)
    sent = message(HALF)
    window = pltpu.VMEM((WIDE, width), BF16)
    window_flops = 2 * ROWS * WIDE * width

    hg, sq, up1, down1 = pl.pallas_call(
        first_kernel,
        in_specs=[far(), far(), far()],
        out_specs=[whole()] * 4,
        out_shape=(pltpu.VMEM((ROWS, width), BF16), pltpu.VMEM((ROWS, 128), F32), sent, sent),
        scratch_shapes=[
            pltpu.VMEM((ROWS, width), BF16),
            pltpu.VMEM((1, width), F32),
            window,
            pltpu.SemaphoreType.DMA((4,)),
        ],
        compiler_params=vmem(12),
        cost_estimate=cost(window_flops, 10_000_000),
        name="first_window",
    )(hidden_states, gain, weights)

    def shifted(array, k):
        return lax.ppermute(array, "dp", [(i, (i + k) % DP) for i in range(DP)])

    up1_in, down1_in = shifted(up1, 1), shifted(down1, -1)
    up2, down2, w_up, w_down = pl.pallas_call(
        direct_kernel,
        in_specs=[whole()] * 2 + [far()],
        out_specs=[whole()] * 4,
        out_shape=(sent, sent, window, window),
        scratch_shapes=[pltpu.SemaphoreType.DMA((2,))],
        compiler_params=vmem(8),
        cost_estimate=cost(window_flops, 10_000_000),
        name="direct_windows",
    )(hg, sq, weights)
    up2_in, down2_in = shifted(up2, 1), shifted(down2, -1)
    *passing, w_own = pl.pallas_call(
        passing_kernel,
        in_specs=[whole()] * 6 + [far()],
        out_specs=[whole()] * 5,
        out_shape=(message(EARLY),) * 2 + (message(HALF - EARLY),) * 2 + (window,),
        scratch_shapes=[pltpu.SemaphoreType.DMA((1,))],
        compiler_params=vmem(8),
        cost_estimate=cost(window_flops, 10_000_000),
        name="passing_windows",
    )(hg, sq, w_up, w_down, up1_in, down1_in, weights)
    up3a, down3a, up3b, down3b = (shifted(array, k) for array, k in zip(passing, (1, -1, 1, -1)))

    own = pl.pallas_call(
        own_kernel,
        in_specs=[whole()] * 2,
        out_specs=whole(),
        out_shape=pltpu.VMEM((ROWS, WIDE), F32),
        compiler_params=vmem(8),
        cost_estimate=cost(window_flops, 6_000_000),
        name="own_window",
    )(hg, w_own)
    sums, part, target = pl.pallas_call(
        part_kernel,
        in_specs=[whole()] * 5,
        out_specs=[whole()] * 3,
        out_shape=(pltpu.VMEM((ROWS, WIDE), F32), pltpu.VMEM((ROWS, 128), F32), pltpu.VMEM((ROWS, 128), jnp.int32)),
        compiler_params=vmem(10),
        cost_estimate=cost(4 * ROWS * WIDE, 5_000_000),
        name="own_and_direct",
    )(ids, sq, own, up2_in, down2_in)

    early, early_rows = pl.pallas_call(
        early_kernel,
        in_specs=[whole()] * 5,
        out_specs=[whole()] * 2,
        out_shape=(pltpu.VMEM((2 * EARLY, WIDE), F32), shape(16, 128)),
        scratch_shapes=totals_scratch(EARLY),
        compiler_params=vmem(8),
        name="early_totals",
    )(sums, part, target, up3a, down3a)
    late, parts = pl.pallas_call(
        late_kernel,
        in_specs=[whole()] * 6,
        out_specs=[whole()] * 2,
        out_shape=(pltpu.VMEM((ROWS - 2 * EARLY, WIDE), F32), shape(lax.axis_size("tp"), 16, 128)),
        scratch_shapes=totals_scratch(HALF - EARLY),
        compiler_params=vmem(8),
        name="late_totals",
    )(sums, part, target, up3b, down3b, early_rows)
    parts = lax.all_to_all(parts, "tp", 0, 0, tiled=True)
    parts = pl.pallas_call(
        join_kernel,
        in_specs=[whole()],
        out_specs=whole(),
        out_shape=shape(lax.axis_size(("section", "dp")), 8, 128),
        compiler_params=vmem(2),
        name="join_totals",
    )(parts)
    parts = lax.all_to_all(parts, ("section", "dp"), 0, 0, tiled=True)
    logprobs, target = pl.pallas_call(
        last_kernel,
        in_specs=[whole()] * 3,
        out_specs=[far(), whole()],
        out_shape=(shape(ROWS, OWN, dtype=BF16), shape(1, ROWS // DP)),
        scratch_shapes=[pltpu.VMEM((ROWS, OWN), BF16), pltpu.VMEM((8, 128), F32), pltpu.VMEM((ROWS, 1), F32), pltpu.SemaphoreType.DMA((DP,))],
        compiler_params=vmem(8),
        name="log_probabilities",
    )(early, late, parts)
    return logprobs, target.reshape(ROWS // DP)


def solution(mesh):
    placed = (P(None, "dp"), P("dp"), P("dp", ("section", "tp")), P())
    return jax.shard_map(
        body,
        mesh=mesh,
        in_specs=placed,
        out_specs=(P(None, ("section", "tp", "dp")), P("dp")),
        check_vma=False,
    )
```

```python
import jax
import jax.numpy as jnp
from jax import lax
from jax.experimental import pallas as pl
from jax.experimental.pallas import tpu as pltpu
from jax.sharding import PartitionSpec as P

D = 8192
EPSILON = 1e-06
ROWS = 672
HALF = ROWS // 2
QUARTER = ROWS // 4
FREE = QUARTER - 128
EARLY = 240
DP = 4
OWN = 594
STEP = 592
SPAN = 600
WIDE = 640
LAST = 512
OVER = OWN - LAST
PLACE = 3 * OVER - 128
BLOCK = 112
PIECE = 48
F32 = jnp.float32
BF16 = jnp.bfloat16
CONTRACT = (((1,), (1,)), ((), ()))


def whole():
    return pl.BlockSpec(memory_space=pltpu.VMEM)


def far():
    return pl.BlockSpec(memory_space=pltpu.HBM)


def vmem(mib):
    return pltpu.CompilerParams(vmem_limit_bytes=mib * 1024 * 1024)


def shape(*dims, dtype=F32):
    return jax.ShapeDtypeStruct(dims, dtype)


def cost(flops, nbytes):
    return pl.CostEstimate(flops=flops, bytes_accessed=nbytes, transcendentals=0)


def lane_of(dims):
    return lax.broadcasted_iota(jnp.int32, dims, 1)


def row_of(dims):
    return lax.broadcasted_iota(jnp.int32, dims, 0)


def to_lanes(column, begin=0):
    dims = (column.shape[0], 128)
    return jnp.sum(jnp.where(row_of(dims) + begin == lane_of(dims), column, 0.0), axis=0, keepdims=True)


def to_column(row, n=128):
    return jnp.sum(jnp.where(row_of((n, 128)) == lane_of((n, 128)), row, 0.0), axis=1, keepdims=True)


def lane_groups():
    return [(k, begin, min(128, ROWS - begin)) for k, begin in enumerate(range(0, ROWS, 128))]


def window_copy(w_ref, chunk, held_ref, sem):
    rows = pl.ds(pl.multiple_of(lax.rem(chunk, DP) * STEP, 16), SPAN)
    return pltpu.make_async_copy(w_ref.at[rows], held_ref.at[pl.ds(0, SPAN)], sem)


def dot(left, right):
    return lax.dot_general(left, right, CONTRACT, preferred_element_type=F32)


def message(rows):
    return pltpu.VMEM((rows + rows // 6, LAST), BF16)


def pack(out_ref, logits, squares):
    n = logits.shape[0]
    third, sixth = n // 3, n // 6
    out_ref[:n, :] = logits[:, :LAST].astype(BF16)
    over = [logits[k * third : k * third + third, LAST:] for k in range(3)]
    lane = lane_of((third, 128))
    middle = pltpu.roll(over[1], OVER, 1)
    first = jnp.where(lane < OVER, over[0], middle)
    second = jnp.where(lane < 2 * OVER - 128, middle, pltpu.roll(over[2], 2 * OVER - 128, 1))
    for k in range(3):
        total = squares[k * third : k * third + third]
        high = total.astype(BF16).astype(F32)
        mid = (total - high).astype(BF16).astype(F32)
        for place, term in enumerate((high, mid, total - high - mid)):
            second = jnp.where(lane == PLACE + 3 * k + place, term, second)
    second = jnp.where(lane < PLACE + 9, second, 0.0)
    for i in (0, 1):
        for j, tile in enumerate((first, second)):
            begin = 256 * i + 128 * j
            out_ref[n:, begin : begin + 128] = tile[i * sixth : i * sixth + sixth].astype(BF16)


def unpack(in_ref, n):
    third = n // 3
    rest = in_ref[n : n + n // 6, :].astype(F32)
    first = jnp.concatenate([rest[:, 0:128], rest[:, 256:384]], axis=0)
    second = jnp.concatenate([rest[:, 128:256], rest[:, 384:512]], axis=0)
    lane = lane_of((third, 128))
    middle = jnp.where(lane < 128 - OVER, pltpu.roll(first, 128 - OVER, 1), pltpu.roll(second, 128 - OVER, 1))
    over = jnp.concatenate([first, middle, pltpu.roll(second, 2 * (128 - OVER), 1)], axis=0)
    squares = []
    for k in range(3):
        held = (lane >= PLACE + 3 * k) & (lane < PLACE + 3 * k + 3)
        squares.append(jnp.sum(jnp.where(held, second, 0.0), axis=1, keepdims=True))
    return over, jnp.concatenate(squares, axis=0)


def aligned(logits, offset):
    shift = (OWN - STEP) * lax.rem(lax.axis_index("dp") + offset, DP)
    moved = [pltpu.roll(logits[:, k : k + 128], lax.rem(128 - shift, 128), 1) for k in range(0, WIDE, 128)]
    stays = lane_of(moved[0].shape) < 128 - shift
    whole_tiles = [jnp.where(stays, tile, after) for tile, after in zip(moved, moved[1:])]
    return jnp.concatenate(whole_tiles + moved[-1:], axis=1)


def scaled(x, g_ref, hg_ref, sq_ref, at):
    for begin in range(at, at + HALF, PIECE):
        rows = slice(begin, begin + PIECE)
        total = jnp.zeros((PIECE, 128), F32)
        for k in range(0, x.shape[1], 128):
            part = x[rows, k : k + 128].astype(F32)
            hg_ref[rows, k : k + 128] = (part * g_ref[:, k : k + 128]).astype(BF16)
            total = total + part * part
        sq_ref[rows, :] = jnp.broadcast_to(jnp.sum(total, axis=1, keepdims=True), (PIECE, 128))


def first_kernel(x_ref, g_ref, w_ref, hg_ref, sq_ref, up_ref, down_ref, x_held, g_held, w_held, sem):
    g_copy = pltpu.make_async_copy(g_ref, g_held, sem.at[0])
    w_copy = window_copy(w_ref, lax.axis_index("dp") + 2, w_held, sem.at[1])
    x_copies = []
    for half in (0, 1):
        rows = pl.ds(half * HALF, HALF)
        x_copies.append(pltpu.make_async_copy(x_ref.at[rows], x_held.at[rows], sem.at[2 + half]))
    for copy in [g_copy, *x_copies, w_copy]:
        copy.start()
    g_copy.wait()
    for half in (0, 1):
        x_copies[half].wait()
        scaled(x_held, g_held, hg_ref, sq_ref, half * HALF)
    w_copy.wait()
    for half, out_ref in ((0, up_ref), (1, down_ref)):
        rows = slice(half * HALF, half * HALF + HALF)
        pack(out_ref, aligned(dot(hg_ref[rows, :], w_held[...]), 2), sq_ref[rows, :])


def direct_kernel(hg_ref, sq_ref, w_ref, up_ref, down_ref, w_up_ref, w_down_ref, sem):
    copies = []
    for i, held_ref in enumerate((w_up_ref, w_down_ref)):
        copies.append(window_copy(w_ref, lax.axis_index("dp") + 1 + 2 * i, held_ref, sem.at[i]))
        copies[-1].start()
    for copy in copies:
        copy.wait()
    for i, (held_ref, out_ref) in enumerate(((w_up_ref, up_ref), (w_down_ref, down_ref))):
        rows = slice(HALF - i * HALF, ROWS - i * HALF)
        pack(out_ref, aligned(dot(hg_ref[rows, :], held_ref[...]), 1 + 2 * i), sq_ref[rows, :])


def passing_kernel(hg_ref, sq_ref, w_up_ref, w_down_ref, up_in_ref, down_in_ref, w_ref, *outs):
    outs, (w_own_ref, sem) = outs[:4], outs[4:]
    copy = window_copy(w_ref, lax.axis_index("dp"), w_own_ref, sem.at[0])
    copy.start()
    for i, (held_ref, in_ref) in enumerate(((w_up_ref, up_in_ref), (w_down_ref, down_in_ref))):
        rows = slice(i * HALF, i * HALF + HALF)
        over, squares = unpack(in_ref, HALF)
        came = jnp.concatenate([in_ref[:HALF, :].astype(F32), over], axis=1)
        total = sq_ref[rows, :] + squares
        logits = aligned(dot(hg_ref[rows, :], held_ref[...]), 1 + 2 * i) + came
        for k, part in ((0, slice(0, EARLY)), (1, slice(EARLY, HALF))):
            pack(outs[2 * k + i], logits[part], total[part])
    copy.wait()


def own_kernel(hg_ref, w_own_ref, own_ref):
    own_ref[...] = dot(hg_ref[...], w_own_ref[...])


def part_kernel(ids_ref, sq_ref, own_ref, up_ref, down_ref, sum_ref, part_ref, target_ref):
    group = lax.axis_index("section") * lax.axis_size("tp") + lax.axis_index("tp")
    base = (group * DP + lax.axis_index("dp")) * OWN
    for k, begin, n in lane_groups():
        same = row_of((n, n)) == lane_of((n, n))
        ids = jnp.sum(jnp.where(same, ids_ref[:, begin : begin + n].astype(F32), 0.0), axis=1, keepdims=True)
        target = ids.astype(jnp.int32) - base
        target_ref[begin : begin + n, :] = jnp.broadcast_to(jnp.where(target < OWN, target, -1), (n, 128))
    for half, came_ref in ((0, down_ref), (1, up_ref)):
        over, squares = unpack(came_ref, HALF)
        part_ref[half * HALF : half * HALF + HALF, :] = sq_ref[half * HALF : half * HALF + HALF, :] + squares
        for begin in range(0, HALF, BLOCK):
            rows, part = slice(half * HALF + begin, half * HALF + begin + BLOCK), slice(begin, begin + BLOCK)
            own = aligned(own_ref[rows, :], 0)
            sum_ref[rows, :LAST] = own[:, :LAST] + came_ref[part, :].astype(F32)
            sum_ref[rows, LAST:] = own[:, LAST:] + over[part]


def block_totals(at, n, sum_ref, part_ref, target_ref, came_ref, logits_ref, to, over_ref, scale_ref, lse_ref, picked_ref):
    over, squares = unpack(came_ref, n)
    over_ref[...] = over
    scale_ref[...] = lax.rsqrt((part_ref[at : at + n, :] + squares) / D + EPSILON)
    for begin in range(0, n, PIECE):
        rows, part, out = (slice(start + begin, start + begin + PIECE) for start in (at, 0, to))
        lane = lane_of((PIECE, 128))
        scale, target = scale_ref[part, :], target_ref[rows, :]
        tiles = []
        for k in range(0, WIDE, 128):
            came = over_ref[part, :] if k == LAST else came_ref[part, k : k + 128].astype(F32)
            tile = (sum_ref[rows, k : k + 128] + came) * scale
            logits_ref[out, k : k + 128] = tile
            tiles.append(jnp.where(lane < OVER, tile, -jnp.inf) if k == LAST else tile)
        top = tiles[0]
        for tile in tiles[1:]:
            top = jnp.maximum(top, tile)
        top = jnp.max(top, axis=1, keepdims=True)
        total = picked = jnp.zeros((PIECE, 128), F32)
        for k, tile in enumerate(tiles):
            total = total + jnp.exp(tile - top)
            picked = picked + jnp.where(lane == target - 128 * k, tile, 0.0)
        lse_ref[part, :] = top + jnp.log(jnp.sum(total, axis=1, keepdims=True))
        picked_ref[part, :] = jnp.sum(picked, axis=1, keepdims=True)


def totals_scratch(n):
    return [pltpu.VMEM((2, n, lanes), F32) for lanes in (128, 128, 1, 1)]


def early_kernel(sum_ref, part_ref, target_ref, up_ref, down_ref, logits_ref, out_ref, *scratch):
    out_ref[...] = jnp.zeros(out_ref.shape, F32)
    for half, came_ref in ((0, up_ref), (1, down_ref)):
        held = [ref.at[half] for ref in scratch]
        block_totals(half * HALF, EARLY, sum_ref, part_ref, target_ref, came_ref, logits_ref, half * EARLY, *held)
        for first, column in zip((4 * half, 8 + 4 * half), held[2:]):
            for k, (begin, end) in enumerate(((0, 128), (128, QUARTER), (QUARTER, EARLY))):
                out_ref[first + k : first + k + 1, :] = to_lanes(column[begin:end, :])


def late_kernel(sum_ref, part_ref, target_ref, up_ref, down_ref, early_ref, logits_ref, out_ref, *scratch):
    late = HALF - EARLY
    row = row_of(early_ref.shape)
    rows = early_ref[...]
    for half, came_ref in ((0, up_ref), (1, down_ref)):
        held = [ref.at[half] for ref in scratch]
        block_totals(half * HALF + EARLY, late, sum_ref, part_ref, target_ref, came_ref, logits_ref, half * late, *held)
        for first, column in zip((4 * half, 8 + 4 * half), held[2:]):
            begun = EARLY - QUARTER
            rows = jnp.where(row == first + 2, rows + to_lanes(column[: 128 - begun, :], begun), rows)
            rows = jnp.where(row == first + 3, to_lanes(column[128 - begun :, :]), rows)
    out_ref[...] = jnp.broadcast_to(rows[None], out_ref.shape)


def join_kernel(parts_ref, out_ref):
    lse = joined(parts_ref[:, :8, :])
    picked = jnp.sum(parts_ref[:, 8:, :], axis=0)
    row, lane = row_of((8, 128)), lane_of((8, 128))
    for k in range(DP):
        first, second = (jnp.broadcast_to(picked[2 * k + i : 2 * k + i + 1, :], (8, 128)) for i in (0, 1))
        both = jnp.where((row == 1) & (lane >= FREE), pltpu.roll(first, FREE, 1), lse)
        both = jnp.where((row == 3) & (lane >= FREE), pltpu.roll(first, 2 * FREE, 1), both)
        both = jnp.where((row == 5) & (lane >= FREE), pltpu.roll(second, FREE, 1), both)
        for part in range(k, out_ref.shape[0], DP):
            out_ref[part, :, :] = both


def joined(parts):
    top = jnp.max(parts, axis=0)
    return top + jnp.log(jnp.sum(jnp.exp(parts - top[None]), axis=0))


def last_kernel(early_ref, late_ref, parts_ref, out_ref, target_ref, out_held, lse_held, out_sem):
    parts = parts_ref[...]
    lse = joined(parts)
    lse_held[...] = lse
    copies = []
    pieces = [(begin, 32, 0, begin) for begin in range(0, 128, 32)]
    pieces += [(128, FREE, 1, 0), (QUARTER, 40, 2, 0), (QUARTER + 40, 32, 2, 40)]
    pieces += [(EARLY, 32, 2, 72), (EARLY + 32, 24, 2, 104), (QUARTER + 128, FREE, 3, 0)]
    for half in (0, 1):
        for begin, n, row, lane in pieces:
            same = row_of((n, 128)) + lane == lane_of((n, 128))
            column = jnp.sum(jnp.where(same, lse[4 * half + row : 4 * half + row + 1, :], 0.0), axis=1, keepdims=True)
            held, size, at = (early_ref, EARLY, begin) if begin < EARLY else (late_ref, HALF - EARLY, begin - EARLY)
            logits = held[half * size + at : half * size + at + n, :]
            out = half * HALF + begin
            out_held[out : out + n, :] = (logits - column)[:, :OWN].astype(BF16)
            if begin + n in (EARLY, HALF):
                first = half * HALF + (0 if begin < EARLY else EARLY)
                rows = pl.ds(first, out + n - first)
                copies.append(pltpu.make_async_copy(out_held.at[rows], out_ref.at[rows], out_sem.at[len(copies)]))
                copies[-1].start()
    picked = jnp.sum(parts, axis=0)
    lane = lane_of((1, 128))
    first = jnp.where(lane < 128 - FREE, pltpu.roll(picked[1:2, :], 128 - FREE, 1), pltpu.roll(picked[3:4, :], 128 - 2 * FREE, 1))
    second = pltpu.roll(picked[5:6, :], 128 - FREE, 1)
    place = 2 * lax.axis_index("dp")
    target_ref[:, 0:128] = first - lse_held[pl.ds(place, 1), :]
    target_ref[:, 128:QUARTER] = (second - lse_held[pl.ds(place + 1, 1), :])[:, : QUARTER - 128]
    for copy in copies:
        copy.wait()


def body(hidden_states, norm_gain, lm_head, target_ids):
    width = hidden_states.shape[1]
    hidden_states = pltpu.with_memory_space_constraint(hidden_states, pltpu.HBM)
    weights = pltpu.with_memory_space_constraint(lm_head.T, pltpu.HBM)
    gain = pltpu.with_memory_space_constraint(norm_gain.reshape(1, width), pltpu.HBM)
    ids = target_ids.reshape(1, ROWS)
    sent = message(HALF)
    window = pltpu.VMEM((WIDE, width), BF16)
    window_flops = 2 * ROWS * WIDE * width

    hg, sq, up1, down1 = pl.pallas_call(
        first_kernel,
        in_specs=[far(), far(), far()],
        out_specs=[whole()] * 4,
        out_shape=(pltpu.VMEM((ROWS, width), BF16), pltpu.VMEM((ROWS, 128), F32), sent, sent),
        scratch_shapes=[
            pltpu.VMEM((ROWS, width), BF16),
            pltpu.VMEM((1, width), F32),
            window,
            pltpu.SemaphoreType.DMA((4,)),
        ],
        compiler_params=vmem(12),
        cost_estimate=cost(window_flops, 10_000_000),
        name="first_window",
    )(hidden_states, gain, weights)

    def shifted(array, k):
        return lax.ppermute(array, "dp", [(i, (i + k) % DP) for i in range(DP)])

    up1_in, down1_in = shifted(up1, 1), shifted(down1, -1)
    up2, down2, w_up, w_down = pl.pallas_call(
        direct_kernel,
        in_specs=[whole()] * 2 + [far()],
        out_specs=[whole()] * 4,
        out_shape=(sent, sent, window, window),
        scratch_shapes=[pltpu.SemaphoreType.DMA((2,))],
        compiler_params=vmem(8),
        cost_estimate=cost(window_flops, 10_000_000),
        name="direct_windows",
    )(hg, sq, weights)
    up2_in, down2_in = shifted(up2, 1), shifted(down2, -1)
    *passing, w_own = pl.pallas_call(
        passing_kernel,
        in_specs=[whole()] * 6 + [far()],
        out_specs=[whole()] * 5,
        out_shape=(message(EARLY),) * 2 + (message(HALF - EARLY),) * 2 + (window,),
        scratch_shapes=[pltpu.SemaphoreType.DMA((1,))],
        compiler_params=vmem(8),
        cost_estimate=cost(window_flops, 10_000_000),
        name="passing_windows",
    )(hg, sq, w_up, w_down, up1_in, down1_in, weights)
    up3a, down3a, up3b, down3b = (shifted(array, k) for array, k in zip(passing, (1, -1, 1, -1)))

    own = pl.pallas_call(
        own_kernel,
        in_specs=[whole()] * 2,
        out_specs=whole(),
        out_shape=pltpu.VMEM((ROWS, WIDE), F32),
        compiler_params=vmem(8),
        cost_estimate=cost(window_flops, 6_000_000),
        name="own_window",
    )(hg, w_own)
    sums, part, target = pl.pallas_call(
        part_kernel,
        in_specs=[whole()] * 5,
        out_specs=[whole()] * 3,
        out_shape=(pltpu.VMEM((ROWS, WIDE), F32), pltpu.VMEM((ROWS, 128), F32), pltpu.VMEM((ROWS, 128), jnp.int32)),
        compiler_params=vmem(10),
        cost_estimate=cost(4 * ROWS * WIDE, 5_000_000),
        name="own_and_direct",
    )(ids, sq, own, up2_in, down2_in)

    early, early_rows = pl.pallas_call(
        early_kernel,
        in_specs=[whole()] * 5,
        out_specs=[whole()] * 2,
        out_shape=(pltpu.VMEM((2 * EARLY, WIDE), F32), shape(16, 128)),
        scratch_shapes=totals_scratch(EARLY),
        compiler_params=vmem(8),
        name="early_totals",
    )(sums, part, target, up3a, down3a)
    late, parts = pl.pallas_call(
        late_kernel,
        in_specs=[whole()] * 6,
        out_specs=[whole()] * 2,
        out_shape=(pltpu.VMEM((ROWS - 2 * EARLY, WIDE), F32), shape(lax.axis_size("tp"), 16, 128)),
        scratch_shapes=totals_scratch(HALF - EARLY),
        compiler_params=vmem(8),
        name="late_totals",
    )(sums, part, target, up3b, down3b, early_rows)
    parts = lax.all_to_all(parts, "tp", 0, 0, tiled=True)
    parts = pl.pallas_call(
        join_kernel,
        in_specs=[whole()],
        out_specs=whole(),
        out_shape=shape(lax.axis_size(("section", "dp")), 8, 128),
        compiler_params=vmem(2),
        name="join_totals",
    )(parts)
    parts = lax.all_to_all(parts, ("section", "dp"), 0, 0, tiled=True)
    logprobs, target = pl.pallas_call(
        last_kernel,
        in_specs=[whole()] * 3,
        out_specs=[far(), whole()],
        out_shape=(shape(ROWS, OWN, dtype=BF16), shape(1, ROWS // DP)),
        scratch_shapes=[pltpu.VMEM((ROWS, OWN), BF16), pltpu.VMEM((8, 128), F32), pltpu.SemaphoreType.DMA((DP,))],
        compiler_params=vmem(8),
        name="log_probabilities",
    )(early, late, parts)
    return logprobs, target.reshape(ROWS // DP)


def solution(mesh):
    placed = (P(None, "dp"), P("dp"), P("dp", ("section", "tp")), P())
    return jax.shard_map(
        body,
        mesh=mesh,
        in_specs=placed,
        out_specs=(P(None, ("section", "tp", "dp")), P("dp")),
        check_vma=False,
    )
```

```python
import jax
import jax.numpy as jnp
from jax import lax
from jax.experimental import pallas as pl
from jax.experimental.pallas import tpu as pltpu
from jax.sharding import PartitionSpec as P

D = 8192
EPSILON = 1e-06
ROWS = 672
HALF = ROWS // 2
QUARTER = ROWS // 4
FREE = QUARTER - 128
EARLY = 240
DP = 4
OWN = 594
STEP = 592
SPAN = 600
WIDE = 640
LAST = 512
OVER = OWN - LAST
PLACE = 3 * OVER - 128
BLOCK = 112
PIECE = 48
F32 = jnp.float32
BF16 = jnp.bfloat16
CONTRACT = (((1,), (1,)), ((), ()))


def whole():
    return pl.BlockSpec(memory_space=pltpu.VMEM)


def far():
    return pl.BlockSpec(memory_space=pltpu.HBM)


def vmem(mib):
    return pltpu.CompilerParams(vmem_limit_bytes=mib * 1024 * 1024)


def shape(*dims, dtype=F32):
    return jax.ShapeDtypeStruct(dims, dtype)


def cost(flops, nbytes):
    return pl.CostEstimate(flops=flops, bytes_accessed=nbytes, transcendentals=0)


def lane_of(dims):
    return lax.broadcasted_iota(jnp.int32, dims, 1)


def row_of(dims):
    return lax.broadcasted_iota(jnp.int32, dims, 0)


def to_lanes(column, begin=0):
    dims = (column.shape[0], 128)
    return jnp.sum(jnp.where(row_of(dims) + begin == lane_of(dims), column, 0.0), axis=0, keepdims=True)


def to_column(row, n=128):
    return jnp.sum(jnp.where(row_of((n, 128)) == lane_of((n, 128)), row, 0.0), axis=1, keepdims=True)


def lane_groups():
    return [(k, begin, min(128, ROWS - begin)) for k, begin in enumerate(range(0, ROWS, 128))]


def window_copy(w_ref, chunk, held_ref, sem):
    rows = pl.ds(pl.multiple_of(lax.rem(chunk, DP) * STEP, 16), SPAN)
    return pltpu.make_async_copy(w_ref.at[rows], held_ref.at[pl.ds(0, SPAN)], sem)


def dot(left, right):
    return lax.dot_general(left, right, CONTRACT, preferred_element_type=F32)


def message(rows):
    return pltpu.VMEM(((rows + rows // 6 + 15) // 16 * 16, LAST), BF16)


def pack(out_ref, logits, squares):
    n = logits.shape[0]
    third, sixth = n // 3, n // 6
    out_ref[:n, :] = logits[:, :LAST].astype(BF16)
    over = [logits[k * third : k * third + third, LAST:] for k in range(3)]
    lane = lane_of((third, 128))
    middle = pltpu.roll(over[1], OVER, 1)
    first = jnp.where(lane < OVER, over[0], middle)
    second = jnp.where(lane < 2 * OVER - 128, middle, pltpu.roll(over[2], 2 * OVER - 128, 1))
    for k in range(3):
        total = squares[k * third : k * third + third]
        high = total.astype(BF16).astype(F32)
        mid = (total - high).astype(BF16).astype(F32)
        for place, term in enumerate((high, mid, total - high - mid)):
            second = jnp.where(lane == PLACE + 3 * k + place, term, second)
    second = jnp.where(lane < PLACE + 9, second, 0.0)
    for i in (0, 1):
        for j, tile in enumerate((first, second)):
            begin = 256 * i + 128 * j
            out_ref[n : n + sixth, begin : begin + 128] = tile[i * sixth : i * sixth + sixth].astype(BF16)


def unpack(in_ref, n):
    third = n // 3
    rest = in_ref[n : n + n // 6, :].astype(F32)
    first = jnp.concatenate([rest[:, 0:128], rest[:, 256:384]], axis=0)
    second = jnp.concatenate([rest[:, 128:256], rest[:, 384:512]], axis=0)
    lane = lane_of((third, 128))
    middle = jnp.where(lane < 128 - OVER, pltpu.roll(first, 128 - OVER, 1), pltpu.roll(second, 128 - OVER, 1))
    over = jnp.concatenate([first, middle, pltpu.roll(second, 2 * (128 - OVER), 1)], axis=0)
    squares = []
    for k in range(3):
        held = (lane >= PLACE + 3 * k) & (lane < PLACE + 3 * k + 3)
        squares.append(jnp.sum(jnp.where(held, second, 0.0), axis=1, keepdims=True))
    return over, jnp.concatenate(squares, axis=0)


def aligned(logits, offset):
    shift = (OWN - STEP) * lax.rem(lax.axis_index("dp") + offset, DP)
    moved = [pltpu.roll(logits[:, k : k + 128], lax.rem(128 - shift, 128), 1) for k in range(0, WIDE, 128)]
    stays = lane_of(moved[0].shape) < 128 - shift
    whole_tiles = [jnp.where(stays, tile, after) for tile, after in zip(moved, moved[1:])]
    return jnp.concatenate(whole_tiles + moved[-1:], axis=1)


def scaled(x, g_ref, hg_ref, sq_ref, at):
    for begin in range(at, at + HALF, PIECE):
        rows = slice(begin, begin + PIECE)
        total = jnp.zeros((PIECE, 128), F32)
        for k in range(0, x.shape[1], 128):
            part = x[rows, k : k + 128].astype(F32)
            hg_ref[rows, k : k + 128] = (part * g_ref[:, k : k + 128]).astype(BF16)
            total = total + part * part
        sq_ref[rows, :] = jnp.broadcast_to(jnp.sum(total, axis=1, keepdims=True), (PIECE, 128))


def first_kernel(x_ref, g_ref, w_ref, hg_ref, sq_ref, up_ref, down_ref, x_held, g_held, w_held, sem):
    g_copy = pltpu.make_async_copy(g_ref, g_held, sem.at[0])
    w_copy = window_copy(w_ref, lax.axis_index("dp") + 2, w_held, sem.at[1])
    x_copies = []
    for half in (0, 1):
        rows = pl.ds(half * HALF, HALF)
        x_copies.append(pltpu.make_async_copy(x_ref.at[rows], x_held.at[rows], sem.at[2 + half]))
    for copy in [g_copy, *x_copies, w_copy]:
        copy.start()
    g_copy.wait()
    for half in (0, 1):
        x_copies[half].wait()
        scaled(x_held, g_held, hg_ref, sq_ref, half * HALF)
    w_copy.wait()
    for half, out_ref in ((0, up_ref), (1, down_ref)):
        rows = slice(half * HALF, half * HALF + HALF)
        pack(out_ref, aligned(dot(hg_ref[rows, :], w_held[...]), 2), sq_ref[rows, :])


def direct_kernel(hg_ref, sq_ref, w_ref, up_ref, down_ref, w_up_ref, w_down_ref, sem):
    copies = []
    for i, held_ref in enumerate((w_up_ref, w_down_ref)):
        copies.append(window_copy(w_ref, lax.axis_index("dp") + 1 + 2 * i, held_ref, sem.at[i]))
        copies[-1].start()
    for copy in copies:
        copy.wait()
    for i, (held_ref, out_ref) in enumerate(((w_up_ref, up_ref), (w_down_ref, down_ref))):
        rows = slice(HALF - i * HALF, ROWS - i * HALF)
        pack(out_ref, aligned(dot(hg_ref[rows, :], held_ref[...]), 1 + 2 * i), sq_ref[rows, :])


def passing_kernel(hg_ref, sq_ref, w_up_ref, w_down_ref, up_in_ref, down_in_ref, w_ref, *outs):
    outs, (w_own_ref, sem) = outs[:4], outs[4:]
    copy = window_copy(w_ref, lax.axis_index("dp"), w_own_ref, sem.at[0])
    copy.start()
    for i, (held_ref, in_ref) in enumerate(((w_up_ref, up_in_ref), (w_down_ref, down_in_ref))):
        rows = slice(i * HALF, i * HALF + HALF)
        over, squares = unpack(in_ref, HALF)
        came = jnp.concatenate([in_ref[:HALF, :].astype(F32), over], axis=1)
        total = sq_ref[rows, :] + squares
        logits = aligned(dot(hg_ref[rows, :], held_ref[...]), 1 + 2 * i) + came
        for k, part in ((0, slice(0, EARLY)), (1, slice(EARLY, HALF))):
            pack(outs[2 * k + i], logits[part], total[part])
    copy.wait()


def own_kernel(hg_ref, w_own_ref, own_ref):
    own_ref[...] = dot(hg_ref[...], w_own_ref[...])


def part_kernel(ids_ref, sq_ref, own_ref, up_ref, down_ref, sum_ref, part_ref, target_ref):
    group = lax.axis_index("section") * lax.axis_size("tp") + lax.axis_index("tp")
    base = (group * DP + lax.axis_index("dp")) * OWN
    for k, begin, n in lane_groups():
        same = row_of((n, n)) == lane_of((n, n))
        ids = jnp.sum(jnp.where(same, ids_ref[:, begin : begin + n].astype(F32), 0.0), axis=1, keepdims=True)
        target = ids.astype(jnp.int32) - base
        target_ref[begin : begin + n, :] = jnp.broadcast_to(jnp.where(target < OWN, target, -1), (n, 128))
    for half, came_ref in ((0, down_ref), (1, up_ref)):
        over, squares = unpack(came_ref, HALF)
        part_ref[half * HALF : half * HALF + HALF, :] = sq_ref[half * HALF : half * HALF + HALF, :] + squares
        for begin in range(0, HALF, BLOCK):
            rows, part = slice(half * HALF + begin, half * HALF + begin + BLOCK), slice(begin, begin + BLOCK)
            own = aligned(own_ref[rows, :], 0)
            sum_ref[rows, :LAST] = own[:, :LAST] + came_ref[part, :].astype(F32)
            sum_ref[rows, LAST:] = own[:, LAST:] + over[part]


def block_totals(at, n, sum_ref, part_ref, target_ref, came_ref, logits_ref, to, over_ref, scale_ref, lse_ref, picked_ref):
    over, squares = unpack(came_ref, n)
    over_ref[...] = over
    scale_ref[...] = lax.rsqrt((part_ref[at : at + n, :] + squares) / D + EPSILON)
    for begin in range(0, n, PIECE):
        rows, part, out = (slice(start + begin, start + begin + PIECE) for start in (at, 0, to))
        lane = lane_of((PIECE, 128))
        scale, target = scale_ref[part, :], target_ref[rows, :]
        tiles = []
        for k in range(0, WIDE, 128):
            came = over_ref[part, :] if k == LAST else came_ref[part, k : k + 128].astype(F32)
            tile = (sum_ref[rows, k : k + 128] + came) * scale
            logits_ref[out, k : k + 128] = tile
            tiles.append(jnp.where(lane < OVER, tile, -jnp.inf) if k == LAST else tile)
        top = tiles[0]
        for tile in tiles[1:]:
            top = jnp.maximum(top, tile)
        top = jnp.max(top, axis=1, keepdims=True)
        total = picked = jnp.zeros((PIECE, 128), F32)
        for k, tile in enumerate(tiles):
            total = total + jnp.exp(tile - top)
            picked = picked + jnp.where(lane == target - 128 * k, tile, 0.0)
        lse_ref[part, :] = top + jnp.log(jnp.sum(total, axis=1, keepdims=True))
        picked_ref[part, :] = jnp.sum(picked, axis=1, keepdims=True)


def totals_scratch(n):
    return [pltpu.VMEM((2, n, lanes), F32) for lanes in (128, 128, 1, 1)]


def early_kernel(sum_ref, part_ref, target_ref, up_ref, down_ref, logits_ref, out_ref, *scratch):
    out_ref[...] = jnp.zeros(out_ref.shape, F32)
    for half, came_ref in ((0, up_ref), (1, down_ref)):
        held = [ref.at[half] for ref in scratch]
        block_totals(half * HALF, EARLY, sum_ref, part_ref, target_ref, came_ref, logits_ref, half * EARLY, *held)
        for first, column in zip((4 * half, 8 + 4 * half), held[2:]):
            for k, (begin, end) in enumerate(((0, 128), (128, QUARTER), (QUARTER, EARLY))):
                out_ref[first + k : first + k + 1, :] = to_lanes(column[begin:end, :])


def late_kernel(sum_ref, part_ref, target_ref, up_ref, down_ref, early_ref, logits_ref, out_ref, *scratch):
    late = HALF - EARLY
    row = row_of(early_ref.shape)
    rows = early_ref[...]
    for half, came_ref in ((0, up_ref), (1, down_ref)):
        held = [ref.at[half] for ref in scratch]
        block_totals(half * HALF + EARLY, late, sum_ref, part_ref, target_ref, came_ref, logits_ref, half * late, *held)
        for first, column in zip((4 * half, 8 + 4 * half), held[2:]):
            begun = EARLY - QUARTER
            rows = jnp.where(row == first + 2, rows + to_lanes(column[: 128 - begun, :], begun), rows)
            rows = jnp.where(row == first + 3, to_lanes(column[128 - begun :, :]), rows)
    out_ref[...] = jnp.broadcast_to(rows[None], out_ref.shape)


def join_kernel(parts_ref, out_ref):
    lse = joined(parts_ref[:, :8, :])
    picked = jnp.sum(parts_ref[:, 8:, :], axis=0)
    row, lane = row_of((8, 128)), lane_of((8, 128))
    for k in range(DP):
        first, second = (jnp.broadcast_to(picked[2 * k + i : 2 * k + i + 1, :], (8, 128)) for i in (0, 1))
        both = jnp.where((row == 1) & (lane >= FREE), pltpu.roll(first, FREE, 1), lse)
        both = jnp.where((row == 3) & (lane >= FREE), pltpu.roll(first, 2 * FREE, 1), both)
        both = jnp.where((row == 5) & (lane >= FREE), pltpu.roll(second, FREE, 1), both)
        for part in range(k, out_ref.shape[0], DP):
            out_ref[part, :, :] = both


def joined(parts):
    top = jnp.max(parts, axis=0)
    return top + jnp.log(jnp.sum(jnp.exp(parts - top[None]), axis=0))


def last_kernel(early_ref, late_ref, parts_ref, out_ref, target_ref, out_held, lse_held, out_sem):
    parts = parts_ref[...]
    lse = joined(parts)
    lse_held[...] = lse
    copies = []
    pieces = [(begin, 32, 0, begin) for begin in range(0, 128, 32)]
    pieces += [(128, FREE, 1, 0), (QUARTER, 40, 2, 0), (QUARTER + 40, 32, 2, 40)]
    pieces += [(EARLY, 32, 2, 72), (EARLY + 32, 24, 2, 104), (QUARTER + 128, FREE, 3, 0)]
    for half in (0, 1):
        for begin, n, row, lane in pieces:
            same = row_of((n, 128)) + lane == lane_of((n, 128))
            column = jnp.sum(jnp.where(same, lse[4 * half + row : 4 * half + row + 1, :], 0.0), axis=1, keepdims=True)
            held, size, at = (early_ref, EARLY, begin) if begin < EARLY else (late_ref, HALF - EARLY, begin - EARLY)
            logits = held[half * size + at : half * size + at + n, :]
            out = half * HALF + begin
            out_held[out : out + n, :] = (logits - column)[:, :OWN].astype(BF16)
            if begin + n in (EARLY, HALF):
                first = half * HALF + (0 if begin < EARLY else EARLY)
                rows = pl.ds(first, out + n - first)
                copies.append(pltpu.make_async_copy(out_held.at[rows], out_ref.at[rows], out_sem.at[len(copies)]))
                copies[-1].start()
    picked = jnp.sum(parts, axis=0)
    lane = lane_of((1, 128))
    first = jnp.where(lane < 128 - FREE, pltpu.roll(picked[1:2, :], 128 - FREE, 1), pltpu.roll(picked[3:4, :], 128 - 2 * FREE, 1))
    second = pltpu.roll(picked[5:6, :], 128 - FREE, 1)
    place = 2 * lax.axis_index("dp")
    target_ref[:, 0:128] = first - lse_held[pl.ds(place, 1), :]
    target_ref[:, 128:QUARTER] = (second - lse_held[pl.ds(place + 1, 1), :])[:, : QUARTER - 128]
    for copy in copies:
        copy.wait()


def body(hidden_states, norm_gain, lm_head, target_ids):
    width = hidden_states.shape[1]
    hidden_states = pltpu.with_memory_space_constraint(hidden_states, pltpu.HBM)
    weights = pltpu.with_memory_space_constraint(lm_head.T, pltpu.HBM)
    gain = pltpu.with_memory_space_constraint(norm_gain.reshape(1, width), pltpu.HBM)
    ids = target_ids.reshape(1, ROWS)
    sent = message(HALF)
    window = pltpu.VMEM((WIDE, width), BF16)
    window_flops = 2 * ROWS * WIDE * width

    hg, sq, up1, down1 = pl.pallas_call(
        first_kernel,
        in_specs=[far(), far(), far()],
        out_specs=[whole()] * 4,
        out_shape=(pltpu.VMEM((ROWS, width), BF16), pltpu.VMEM((ROWS, 128), F32), sent, sent),
        scratch_shapes=[
            pltpu.VMEM((ROWS, width), BF16),
            pltpu.VMEM((1, width), F32),
            window,
            pltpu.SemaphoreType.DMA((4,)),
        ],
        compiler_params=vmem(12),
        cost_estimate=cost(window_flops, 10_000_000),
        name="first_window",
    )(hidden_states, gain, weights)

    def shifted(array, k):
        return lax.ppermute(array, "dp", [(i, (i + k) % DP) for i in range(DP)])

    up1_in, down1_in = shifted(up1, 1), shifted(down1, -1)
    up2, down2, w_up, w_down = pl.pallas_call(
        direct_kernel,
        in_specs=[whole()] * 2 + [far()],
        out_specs=[whole()] * 4,
        out_shape=(sent, sent, window, window),
        scratch_shapes=[pltpu.SemaphoreType.DMA((2,))],
        compiler_params=vmem(8),
        cost_estimate=cost(window_flops, 10_000_000),
        name="direct_windows",
    )(hg, sq, weights)
    up2_in, down2_in = shifted(up2, 1), shifted(down2, -1)
    *passing, w_own = pl.pallas_call(
        passing_kernel,
        in_specs=[whole()] * 6 + [far()],
        out_specs=[whole()] * 5,
        out_shape=(message(EARLY),) * 2 + (message(HALF - EARLY),) * 2 + (window,),
        scratch_shapes=[pltpu.SemaphoreType.DMA((1,))],
        compiler_params=vmem(8),
        cost_estimate=cost(window_flops, 10_000_000),
        name="passing_windows",
    )(hg, sq, w_up, w_down, up1_in, down1_in, weights)
    up3a, down3a, up3b, down3b = (shifted(array, k) for array, k in zip(passing, (1, -1, 1, -1)))

    own = pl.pallas_call(
        own_kernel,
        in_specs=[whole()] * 2,
        out_specs=whole(),
        out_shape=pltpu.VMEM((ROWS, WIDE), F32),
        compiler_params=vmem(8),
        cost_estimate=cost(window_flops, 6_000_000),
        name="own_window",
    )(hg, w_own)
    sums, part, target = pl.pallas_call(
        part_kernel,
        in_specs=[whole()] * 5,
        out_specs=[whole()] * 3,
        out_shape=(pltpu.VMEM((ROWS, WIDE), F32), pltpu.VMEM((ROWS, 128), F32), pltpu.VMEM((ROWS, 128), jnp.int32)),
        compiler_params=vmem(10),
        cost_estimate=cost(4 * ROWS * WIDE, 5_000_000),
        name="own_and_direct",
    )(ids, sq, own, up2_in, down2_in)

    early, early_rows = pl.pallas_call(
        early_kernel,
        in_specs=[whole()] * 5,
        out_specs=[whole()] * 2,
        out_shape=(pltpu.VMEM((2 * EARLY, WIDE), F32), shape(16, 128)),
        scratch_shapes=totals_scratch(EARLY),
        compiler_params=vmem(8),
        name="early_totals",
    )(sums, part, target, up3a, down3a)
    late, parts = pl.pallas_call(
        late_kernel,
        in_specs=[whole()] * 6,
        out_specs=[whole()] * 2,
        out_shape=(pltpu.VMEM((ROWS - 2 * EARLY, WIDE), F32), shape(lax.axis_size("tp"), 16, 128)),
        scratch_shapes=totals_scratch(HALF - EARLY),
        compiler_params=vmem(8),
        name="late_totals",
    )(sums, part, target, up3b, down3b, early_rows)
    parts = lax.all_to_all(parts, "tp", 0, 0, tiled=True)
    parts = pl.pallas_call(
        join_kernel,
        in_specs=[whole()],
        out_specs=whole(),
        out_shape=shape(lax.axis_size(("section", "dp")), 8, 128),
        compiler_params=vmem(2),
        name="join_totals",
    )(parts)
    parts = lax.all_to_all(parts, ("section", "dp"), 0, 0, tiled=True)
    logprobs, target = pl.pallas_call(
        last_kernel,
        in_specs=[whole()] * 3,
        out_specs=[far(), whole()],
        out_shape=(shape(ROWS, OWN, dtype=BF16), shape(1, ROWS // DP)),
        scratch_shapes=[pltpu.VMEM((ROWS, OWN), BF16), pltpu.VMEM((8, 128), F32), pltpu.SemaphoreType.DMA((DP,))],
        compiler_params=vmem(8),
        name="log_probabilities",
    )(early, late, parts)
    return logprobs, target.reshape(ROWS // DP)


def solution(mesh):
    placed = (P(None, "dp"), P("dp"), P("dp", ("section", "tp")), P())
    return jax.shard_map(
        body,
        mesh=mesh,
        in_specs=placed,
        out_specs=(P(None, ("section", "tp", "dp")), P("dp")),
        check_vma=False,
    )
```

```python
import jax
import jax.numpy as jnp
from jax import lax
from jax.experimental import pallas as pl
from jax.experimental.pallas import tpu as pltpu
from jax.sharding import PartitionSpec as P

D = 8192
EPSILON = 1e-06
ROWS = 672
HALF = ROWS // 2
QUARTER = ROWS // 4
FREE = QUARTER - 128
EARLY = 240
DP = 4
OWN = 594
STEP = 592
SPAN = 600
WIDE = 640
LAST = 512
OVER = OWN - LAST
PLACE = 3 * OVER - 128
BLOCK = 112
PIECE = 48
F32 = jnp.float32
BF16 = jnp.bfloat16
CONTRACT = (((1,), (1,)), ((), ()))


def whole():
    return pl.BlockSpec(memory_space=pltpu.VMEM)


def far():
    return pl.BlockSpec(memory_space=pltpu.HBM)


def vmem(mib):
    return pltpu.CompilerParams(vmem_limit_bytes=mib * 1024 * 1024)


def shape(*dims, dtype=F32):
    return jax.ShapeDtypeStruct(dims, dtype)


def cost(flops, nbytes):
    return pl.CostEstimate(flops=flops, bytes_accessed=nbytes, transcendentals=0)


def lane_of(dims):
    return lax.broadcasted_iota(jnp.int32, dims, 1)


def row_of(dims):
    return lax.broadcasted_iota(jnp.int32, dims, 0)


def to_lanes(column, begin=0):
    dims = (column.shape[0], 128)
    return jnp.sum(jnp.where(row_of(dims) + begin == lane_of(dims), column, 0.0), axis=0, keepdims=True)


def to_column(row, n=128):
    return jnp.sum(jnp.where(row_of((n, 128)) == lane_of((n, 128)), row, 0.0), axis=1, keepdims=True)


def lane_groups():
    return [(k, begin, min(128, ROWS - begin)) for k, begin in enumerate(range(0, ROWS, 128))]


def window_copy(w_ref, chunk, held_ref, sem):
    rows = pl.ds(pl.multiple_of(lax.rem(chunk, DP) * STEP, 16), SPAN)
    return pltpu.make_async_copy(w_ref.at[rows], held_ref.at[pl.ds(0, SPAN)], sem)


def dot(left, right):
    return lax.dot_general(left, right, CONTRACT, preferred_element_type=F32)


def message(rows):
    return pltpu.VMEM((rows + rows // 6, LAST), BF16)


def pack(out_ref, logits, squares):
    n = logits.shape[0]
    third, sixth = n // 3, n // 6
    out_ref[:n, :] = logits[:, :LAST].astype(BF16)
    over = [logits[k * third : k * third + third, LAST:] for k in range(3)]
    lane = lane_of((third, 128))
    middle = pltpu.roll(over[1], OVER, 1)
    first = jnp.where(lane < OVER, over[0], middle)
    second = jnp.where(lane < 2 * OVER - 128, middle, pltpu.roll(over[2], 2 * OVER - 128, 1))
    for k in range(3):
        total = squares[k * third : k * third + third]
        high = total.astype(BF16).astype(F32)
        mid = (total - high).astype(BF16).astype(F32)
        for place, term in enumerate((high, mid, total - high - mid)):
            second = jnp.where(lane == PLACE + 3 * k + place, term, second)
    second = jnp.where(lane < PLACE + 9, second, 0.0)
    for i in (0, 1):
        for j, tile in enumerate((first, second)):
            begin = 256 * i + 128 * j
            out_ref[n:, begin : begin + 128] = tile[i * sixth : i * sixth + sixth].astype(BF16)


def unpack(in_ref, n):
    third = n // 3
    rest = in_ref[n : n + n // 6, :].astype(F32)
    first = jnp.concatenate([rest[:, 0:128], rest[:, 256:384]], axis=0)
    second = jnp.concatenate([rest[:, 128:256], rest[:, 384:512]], axis=0)
    lane = lane_of((third, 128))
    middle = jnp.where(lane < 128 - OVER, pltpu.roll(first, 128 - OVER, 1), pltpu.roll(second, 128 - OVER, 1))
    over = jnp.concatenate([first, middle, pltpu.roll(second, 2 * (128 - OVER), 1)], axis=0)
    squares = []
    for k in range(3):
        held = (lane >= PLACE + 3 * k) & (lane < PLACE + 3 * k + 3)
        squares.append(jnp.sum(jnp.where(held, second, 0.0), axis=1, keepdims=True))
    return over, jnp.concatenate(squares, axis=0)


def aligned(logits, offset):
    shift = (OWN - STEP) * lax.rem(lax.axis_index("dp") + offset, DP)
    moved = [pltpu.roll(logits[:, k : k + 128], lax.rem(128 - shift, 128), 1) for k in range(0, WIDE, 128)]
    stays = lane_of(moved[0].shape) < 128 - shift
    whole_tiles = [jnp.where(stays, tile, after) for tile, after in zip(moved, moved[1:])]
    return jnp.concatenate(whole_tiles + moved[-1:], axis=1)


def scaled(x, g_ref, hg_ref, sq_ref, at):
    for begin in range(at, at + HALF, PIECE):
        rows = slice(begin, begin + PIECE)
        total = jnp.zeros((PIECE, 128), F32)
        for k in range(0, x.shape[1], 128):
            part = x[rows, k : k + 128].astype(F32)
            hg_ref[rows, k : k + 128] = (part * g_ref[:, k : k + 128]).astype(BF16)
            total = total + part * part
        sq_ref[rows, :] = jnp.broadcast_to(jnp.sum(total, axis=1, keepdims=True), (PIECE, 128))


def first_kernel(x_ref, g_ref, w_ref, hg_ref, sq_ref, up_ref, down_ref, x_held, g_held, w_held, sem):
    g_copy = pltpu.make_async_copy(g_ref, g_held, sem.at[0])
    w_copy = window_copy(w_ref, lax.axis_index("dp") + 2, w_held, sem.at[1])
    x_copies = []
    for half in (0, 1):
        rows = pl.ds(half * HALF, HALF)
        x_copies.append(pltpu.make_async_copy(x_ref.at[rows], x_held.at[rows], sem.at[2 + half]))
    for copy in [g_copy, *x_copies, w_copy]:
        copy.start()
    g_copy.wait()
    for half in (0, 1):
        x_copies[half].wait()
        scaled(x_held, g_held, hg_ref, sq_ref, half * HALF)
    w_copy.wait()
    for half, out_ref in ((0, up_ref), (1, down_ref)):
        rows = slice(half * HALF, half * HALF + HALF)
        pack(out_ref, aligned(dot(hg_ref[rows, :], w_held[...]), 2), sq_ref[rows, :])


def direct_kernel(hg_ref, sq_ref, w_ref, up_ref, down_ref, w_up_ref, w_down_ref, sem):
    copies = []
    for i, held_ref in enumerate((w_up_ref, w_down_ref)):
        copies.append(window_copy(w_ref, lax.axis_index("dp") + 1 + 2 * i, held_ref, sem.at[i]))
        copies[-1].start()
    for copy in copies:
        copy.wait()
    for i, (held_ref, out_ref) in enumerate(((w_up_ref, up_ref), (w_down_ref, down_ref))):
        rows = slice(HALF - i * HALF, ROWS - i * HALF)
        pack(out_ref, aligned(dot(hg_ref[rows, :], held_ref[...]), 1 + 2 * i), sq_ref[rows, :])


def passing_kernel(hg_ref, sq_ref, w_up_ref, w_down_ref, up_in_ref, down_in_ref, w_ref, *outs):
    outs, (w_own_ref, sem) = outs[:4], outs[4:]
    copy = window_copy(w_ref, lax.axis_index("dp"), w_own_ref, sem.at[0])
    copy.start()
    for i, (held_ref, in_ref) in enumerate(((w_up_ref, up_in_ref), (w_down_ref, down_in_ref))):
        rows = slice(i * HALF, i * HALF + HALF)
        over, squares = unpack(in_ref, HALF)
        came = jnp.concatenate([in_ref[:HALF, :].astype(F32), over], axis=1)
        total = sq_ref[rows, :] + squares
        logits = aligned(dot(hg_ref[rows, :], held_ref[...]), 1 + 2 * i) + came
        for k, part in ((0, slice(0, EARLY)), (1, slice(EARLY, HALF))):
            pack(outs[2 * k + i], logits[part], total[part])
    copy.wait()


def own_kernel(hg_ref, w_own_ref, own_ref):
    own_ref[...] = dot(hg_ref[...], w_own_ref[...])


def part_kernel(ids_ref, sq_ref, own_ref, up_ref, down_ref, sum_ref, part_ref, target_ref):
    group = lax.axis_index("section") * lax.axis_size("tp") + lax.axis_index("tp")
    base = (group * DP + lax.axis_index("dp")) * OWN
    for k, begin, n in lane_groups():
        same = row_of((n, n)) == lane_of((n, n))
        ids = jnp.sum(jnp.where(same, ids_ref[:, begin : begin + n].astype(F32), 0.0), axis=1, keepdims=True)
        target = ids.astype(jnp.int32) - base
        target_ref[begin : begin + n, :] = jnp.broadcast_to(jnp.where(target < OWN, target, -1), (n, 128))
    for half, came_ref in ((0, down_ref), (1, up_ref)):
        over, squares = unpack(came_ref, HALF)
        part_ref[half * HALF : half * HALF + HALF, :] = sq_ref[half * HALF : half * HALF + HALF, :] + squares
        for begin in range(0, HALF, BLOCK):
            rows, part = slice(half * HALF + begin, half * HALF + begin + BLOCK), slice(begin, begin + BLOCK)
            own = aligned(own_ref[rows, :], 0)
            sum_ref[rows, :LAST] = own[:, :LAST] + came_ref[part, :].astype(F32)
            sum_ref[rows, LAST:] = own[:, LAST:] + over[part]


def block_totals(at, n, sum_ref, part_ref, target_ref, came_ref, logits_ref, to, over_ref, scale_ref, lse_ref, picked_ref):
    over, squares = unpack(came_ref, n)
    over_ref[...] = over
    scale_ref[...] = lax.rsqrt((part_ref[at : at + n, :] + squares) / D + EPSILON)
    piece = 80 if n == EARLY else 96
    for begin in range(0, n, piece):
        rows, part, out = (slice(start + begin, start + begin + piece) for start in (at, 0, to))
        lane = lane_of((piece, 128))
        scale, target = scale_ref[part, :], target_ref[rows, :]
        tiles = []
        for k in range(0, WIDE, 128):
            came = over_ref[part, :] if k == LAST else came_ref[part, k : k + 128].astype(F32)
            tile = (sum_ref[rows, k : k + 128] + came) * scale
            logits_ref[out, k : k + 128] = tile
            tiles.append(jnp.where(lane < OVER, tile, -jnp.inf) if k == LAST else tile)
        top = tiles[0]
        for tile in tiles[1:]:
            top = jnp.maximum(top, tile)
        top = jnp.max(top, axis=1, keepdims=True)
        total = picked = jnp.zeros((piece, 128), F32)
        for k, tile in enumerate(tiles):
            total = total + jnp.exp(tile - top)
            picked = picked + jnp.where(lane == target - 128 * k, tile, 0.0)
        lse_ref[part, :] = top + jnp.log(jnp.sum(total, axis=1, keepdims=True))
        picked_ref[part, :] = jnp.sum(picked, axis=1, keepdims=True)


def totals_scratch(n):
    return [pltpu.VMEM((2, n, lanes), F32) for lanes in (128, 128, 1, 1)]


def early_kernel(sum_ref, part_ref, target_ref, up_ref, down_ref, logits_ref, out_ref, *scratch):
    out_ref[...] = jnp.zeros(out_ref.shape, F32)
    for half, came_ref in ((0, up_ref), (1, down_ref)):
        held = [ref.at[half] for ref in scratch]
        block_totals(half * HALF, EARLY, sum_ref, part_ref, target_ref, came_ref, logits_ref, half * EARLY, *held)
        for first, column in zip((4 * half, 8 + 4 * half), held[2:]):
            for k, (begin, end) in enumerate(((0, 128), (128, QUARTER), (QUARTER, EARLY))):
                out_ref[first + k : first + k + 1, :] = to_lanes(column[begin:end, :])


def late_kernel(sum_ref, part_ref, target_ref, up_ref, down_ref, early_ref, logits_ref, out_ref, *scratch):
    late = HALF - EARLY
    row = row_of(early_ref.shape)
    rows = early_ref[...]
    for half, came_ref in ((0, up_ref), (1, down_ref)):
        held = [ref.at[half] for ref in scratch]
        block_totals(half * HALF + EARLY, late, sum_ref, part_ref, target_ref, came_ref, logits_ref, half * late, *held)
        for first, column in zip((4 * half, 8 + 4 * half), held[2:]):
            begun = EARLY - QUARTER
            rows = jnp.where(row == first + 2, rows + to_lanes(column[: 128 - begun, :], begun), rows)
            rows = jnp.where(row == first + 3, to_lanes(column[128 - begun :, :]), rows)
    out_ref[...] = jnp.broadcast_to(rows[None], out_ref.shape)


def join_kernel(parts_ref, out_ref):
    lse = joined(parts_ref[:, :8, :])
    picked = jnp.sum(parts_ref[:, 8:, :], axis=0)
    row, lane = row_of((8, 128)), lane_of((8, 128))
    for k in range(DP):
        first, second = (jnp.broadcast_to(picked[2 * k + i : 2 * k + i + 1, :], (8, 128)) for i in (0, 1))
        both = jnp.where((row == 1) & (lane >= FREE), pltpu.roll(first, FREE, 1), lse)
        both = jnp.where((row == 3) & (lane >= FREE), pltpu.roll(first, 2 * FREE, 1), both)
        both = jnp.where((row == 5) & (lane >= FREE), pltpu.roll(second, FREE, 1), both)
        for part in range(k, out_ref.shape[0], DP):
            out_ref[part, :, :] = both


def joined(parts):
    top = jnp.max(parts, axis=0)
    return top + jnp.log(jnp.sum(jnp.exp(parts - top[None]), axis=0))


def last_kernel(early_ref, late_ref, parts_ref, out_ref, target_ref, out_held, lse_held, out_sem):
    parts = parts_ref[...]
    lse = joined(parts)
    lse_held[...] = lse
    copies = []
    pieces = [(begin, 32, 0, begin) for begin in range(0, 128, 32)]
    pieces += [(128, FREE, 1, 0), (QUARTER, 40, 2, 0), (QUARTER + 40, 32, 2, 40)]
    pieces += [(EARLY, 32, 2, 72), (EARLY + 32, 24, 2, 104), (QUARTER + 128, FREE, 3, 0)]
    for half in (0, 1):
        for begin, n, row, lane in pieces:
            same = row_of((n, 128)) + lane == lane_of((n, 128))
            column = jnp.sum(jnp.where(same, lse[4 * half + row : 4 * half + row + 1, :], 0.0), axis=1, keepdims=True)
            held, size, at = (early_ref, EARLY, begin) if begin < EARLY else (late_ref, HALF - EARLY, begin - EARLY)
            logits = held[half * size + at : half * size + at + n, :]
            out = half * HALF + begin
            out_held[out : out + n, :] = (logits - column)[:, :OWN].astype(BF16)
            if begin + n in (EARLY, HALF):
                first = half * HALF + (0 if begin < EARLY else EARLY)
                rows = pl.ds(first, out + n - first)
                copies.append(pltpu.make_async_copy(out_held.at[rows], out_ref.at[rows], out_sem.at[len(copies)]))
                copies[-1].start()
    picked = jnp.sum(parts, axis=0)
    lane = lane_of((1, 128))
    first = jnp.where(lane < 128 - FREE, pltpu.roll(picked[1:2, :], 128 - FREE, 1), pltpu.roll(picked[3:4, :], 128 - 2 * FREE, 1))
    second = pltpu.roll(picked[5:6, :], 128 - FREE, 1)
    place = 2 * lax.axis_index("dp")
    target_ref[:, 0:128] = first - lse_held[pl.ds(place, 1), :]
    target_ref[:, 128:QUARTER] = (second - lse_held[pl.ds(place + 1, 1), :])[:, : QUARTER - 128]
    for copy in copies:
        copy.wait()


def body(hidden_states, norm_gain, lm_head, target_ids):
    width = hidden_states.shape[1]
    hidden_states = pltpu.with_memory_space_constraint(hidden_states, pltpu.HBM)
    weights = pltpu.with_memory_space_constraint(lm_head.T, pltpu.HBM)
    gain = pltpu.with_memory_space_constraint(norm_gain.reshape(1, width), pltpu.HBM)
    ids = target_ids.reshape(1, ROWS)
    sent = message(HALF)
    window = pltpu.VMEM((WIDE, width), BF16)
    window_flops = 2 * ROWS * WIDE * width

    hg, sq, up1, down1 = pl.pallas_call(
        first_kernel,
        in_specs=[far(), far(), far()],
        out_specs=[whole()] * 4,
        out_shape=(pltpu.VMEM((ROWS, width), BF16), pltpu.VMEM((ROWS, 128), F32), sent, sent),
        scratch_shapes=[
            pltpu.VMEM((ROWS, width), BF16),
            pltpu.VMEM((1, width), F32),
            window,
            pltpu.SemaphoreType.DMA((4,)),
        ],
        compiler_params=vmem(12),
        cost_estimate=cost(window_flops, 10_000_000),
        name="first_window",
    )(hidden_states, gain, weights)

    def shifted(array, k):
        return lax.ppermute(array, "dp", [(i, (i + k) % DP) for i in range(DP)])

    up1_in, down1_in = shifted(up1, 1), shifted(down1, -1)
    up2, down2, w_up, w_down = pl.pallas_call(
        direct_kernel,
        in_specs=[whole()] * 2 + [far()],
        out_specs=[whole()] * 4,
        out_shape=(sent, sent, window, window),
        scratch_shapes=[pltpu.SemaphoreType.DMA((2,))],
        compiler_params=vmem(8),
        cost_estimate=cost(window_flops, 10_000_000),
        name="direct_windows",
    )(hg, sq, weights)
    up2_in, down2_in = shifted(up2, 1), shifted(down2, -1)
    *passing, w_own = pl.pallas_call(
        passing_kernel,
        in_specs=[whole()] * 6 + [far()],
        out_specs=[whole()] * 5,
        out_shape=(message(EARLY),) * 2 + (message(HALF - EARLY),) * 2 + (window,),
        scratch_shapes=[pltpu.SemaphoreType.DMA((1,))],
        compiler_params=vmem(8),
        cost_estimate=cost(window_flops, 10_000_000),
        name="passing_windows",
    )(hg, sq, w_up, w_down, up1_in, down1_in, weights)
    up3a, down3a, up3b, down3b = (shifted(array, k) for array, k in zip(passing, (1, -1, 1, -1)))

    own = pl.pallas_call(
        own_kernel,
        in_specs=[whole()] * 2,
        out_specs=whole(),
        out_shape=pltpu.VMEM((ROWS, WIDE), F32),
        compiler_params=vmem(8),
        cost_estimate=cost(window_flops, 6_000_000),
        name="own_window",
    )(hg, w_own)
    sums, part, target = pl.pallas_call(
        part_kernel,
        in_specs=[whole()] * 5,
        out_specs=[whole()] * 3,
        out_shape=(pltpu.VMEM((ROWS, WIDE), F32), pltpu.VMEM((ROWS, 128), F32), pltpu.VMEM((ROWS, 128), jnp.int32)),
        compiler_params=vmem(10),
        cost_estimate=cost(4 * ROWS * WIDE, 5_000_000),
        name="own_and_direct",
    )(ids, sq, own, up2_in, down2_in)

    early, early_rows = pl.pallas_call(
        early_kernel,
        in_specs=[whole()] * 5,
        out_specs=[whole()] * 2,
        out_shape=(pltpu.VMEM((2 * EARLY, WIDE), F32), shape(16, 128)),
        scratch_shapes=totals_scratch(EARLY),
        compiler_params=vmem(8),
        name="early_totals",
    )(sums, part, target, up3a, down3a)
    late, parts = pl.pallas_call(
        late_kernel,
        in_specs=[whole()] * 6,
        out_specs=[whole()] * 2,
        out_shape=(pltpu.VMEM((ROWS - 2 * EARLY, WIDE), F32), shape(lax.axis_size("tp"), 16, 128)),
        scratch_shapes=totals_scratch(HALF - EARLY),
        compiler_params=vmem(8),
        name="late_totals",
    )(sums, part, target, up3b, down3b, early_rows)
    parts = lax.all_to_all(parts, "tp", 0, 0, tiled=True)
    parts = pl.pallas_call(
        join_kernel,
        in_specs=[whole()],
        out_specs=whole(),
        out_shape=shape(lax.axis_size(("section", "dp")), 8, 128),
        compiler_params=vmem(2),
        name="join_totals",
    )(parts)
    parts = lax.all_to_all(parts, ("section", "dp"), 0, 0, tiled=True)
    logprobs, target = pl.pallas_call(
        last_kernel,
        in_specs=[whole()] * 3,
        out_specs=[far(), whole()],
        out_shape=(shape(ROWS, OWN, dtype=BF16), shape(1, ROWS // DP)),
        scratch_shapes=[pltpu.VMEM((ROWS, OWN), BF16), pltpu.VMEM((8, 128), F32), pltpu.SemaphoreType.DMA((DP,))],
        compiler_params=vmem(8),
        name="log_probabilities",
    )(early, late, parts)
    return logprobs, target.reshape(ROWS // DP)


def solution(mesh):
    placed = (P(None, "dp"), P("dp"), P("dp", ("section", "tp")), P())
    return jax.shard_map(
        body,
        mesh=mesh,
        in_specs=placed,
        out_specs=(P(None, ("section", "tp", "dp")), P("dp")),
        check_vma=False,
    )
```
